32 devices in a mesh: fsdp: 8 (over z, x), island: 4 (over y, core).
Axes of the slice: x: 2, y: 2, z: 4, core: 2. Of those that a mesh axis runs over, the one named last changes fastest.
Arguments:
- acts: bfloat16 [4, 2048, 4096], P('island', 'fsdp'), may hold values from -6 to 6
- grad_out: bfloat16 [4, 2048, 128], P('island', 'fsdp'), may hold values from -0.52734375 to 0.52734375
- params: float32 [4, 4096, 128], P('island', 'fsdp'), may hold values from -3 to 3
- adam_m: float32 [4, 4096, 128], P('island', 'fsdp'), may hold values from -4 to 4
- adam_v: float32 [4, 4096, 128], P('island', 'fsdp'), may hold values from 0.01 to 16
- global_params: float32 [4096, 128], P('fsdp'), may hold values from -3 to 3
- outer_mom: float32 [4096, 128], P('fsdp'), may hold values from -2 to 2
Outputs:
- mixed: float32 [4, 4096, 128], P('island', 'fsdp')
- first_moment: float32 [4, 4096, 128], P('island', 'fsdp')
- second_moment: float32 [4, 4096, 128], P('island', 'fsdp')
- new_global: float32 [4096, 128], P('fsdp')
- new_mom: float32 [4096, 128], P('fsdp')
- forward_weight: bfloat16 [4, 4096, 128], P('island')
The draws below stay inside these ranges and needn't reach their ends.
All inputs are finite; a program needn't handle non-finite values.
Results may differ from the reference program's by a relative error of at most 0.0004.
Values may be sent and summed in bfloat16 or wider, within the bound.
A program may use at most 64 MiB of HBM per device.

```python
import math
import jax
import jax.numpy as jnp
from jax import lax

D = 4096
HD = 128
INNER_STEP = 100
ISLANDS = 4
TOKENS = 2048
DP = 4096


def steps_of(rng, extent, cuts, least, largest):
    gain, own = 1.0, jax.random.fold_in(rng, 6)
    for axis_at, blocks in cuts:
        heights = jnp.exp(jax.random.uniform(jax.random.fold_in(own, axis_at), (blocks,), jnp.float32, least / len(cuts), largest / len(cuts)))
        gain = gain * jnp.repeat(heights, extent[axis_at] // blocks).reshape([-1 if axis == axis_at else 1 for axis in range(len(extent))])
    return gain


def centred(own_key, extent, scale, bound, shards=(), kind=jnp.bfloat16):
    result = jax.random.normal(own_key, extent, jnp.float32) * scale
    if len(shards) > 0:
        result = steps_of(own_key, extent, shards, -0.22, 0.18) * result
    return jnp.clip(result, min=-bound, max=bound).astype(kind)


def setup_inputs(seed: int = 0) -> dict:
    key_of = jax.random.split(jax.random.key(seed), 8)
    return {
        "acts": centred(key_of[0], (ISLANDS, TOKENS, D), 1.0, 6.0, ((0, 4), (1, 8))),
        "grad_out": centred(key_of[1], (ISLANDS, TOKENS, HD), (4.0 * TOKENS ** -0.5), 0.52734375, ((0, 4), (1, 8))),
        "params": centred(key_of[2], (ISLANDS, DP, HD), 0.5, 3.0, ((0, 4), (1, 8)), jnp.float32),
        "adam_m": centred(key_of[3], (ISLANDS, DP, HD), 1.0, 4.0, ((0, 4), (1, 8)), jnp.float32),
        "adam_v": jnp.clip(jnp.exp(math.log(16.0) - 7.377759 * jax.random.uniform(key_of[4], (ISLANDS, DP, HD), jnp.float32) ** steps_of(key_of[4], (ISLANDS, DP, HD), ((0, 4), (1, 8)), -0.2, 0.2)), 0.01, 16.0),
        "global_params": centred(key_of[5], (DP, HD), 0.5, 3.0, ((0, 8),), jnp.float32),
        "outer_mom": centred(key_of[6], (DP, HD), 0.3, 2.0, ((0, 8),), jnp.float32),
    }


beta_one = 0.9
beta_two = 0.95
epsilon = 1e-08
inner_rate = 0.001
decay_rate = 0.1
outer_rate = 0.7
momentum = 0.9
mixing = 0.5

def island_gradient(pair):
    inputs, cotangent = pair
    return jnp.dot(inputs.T, cotangent, preferred_element_type=jnp.float32)

def reference(acts, grad_out, params, adam_m, adam_v, global_params, outer_mom):
    gradient = lax.map(island_gradient, (acts, grad_out))
    padding = params.shape[1] - gradient.shape[1]
    gradient = jnp.pad(gradient, ((0, 0), (0, padding), (0, 0)))
    first_moment = beta_one * adam_m + (1.0 - beta_one) * gradient
    second_moment = beta_two * adam_v + (1.0 - beta_two) * gradient * gradient
    first_hat = first_moment / (1.0 - beta_one ** INNER_STEP)
    second_hat = second_moment / (1.0 - beta_two ** INNER_STEP)
    inner = params - inner_rate * (first_hat / (jnp.sqrt(second_hat) + epsilon) + decay_rate * params)
    delta = lax.optimization_barrier(jnp.sum(global_params[None] - inner, axis=0)) / ISLANDS
    new_mom = momentum * outer_mom + delta
    new_global = global_params - outer_rate * (delta + momentum * new_mom)
    mixed = mixing * inner + (1.0 - mixing) * new_global[None]
    forward_weight = mixed[:, :D].astype(jnp.bfloat16)
    return (mixed, first_moment, second_moment, new_global, new_mom, forward_weight)
```

```python
import functools

import jax
import jax.numpy as jnp
from jax import lax
from jax.experimental import pallas as pl
from jax.experimental.pallas import tpu as pltpu
from jax.sharding import PartitionSpec as P

INNER_STEP = 100


beta_one = 0.9
beta_two = 0.95
epsilon = 1e-08
inner_rate = 0.001
decay_rate = 0.1
outer_rate = 0.7
momentum = 0.9
mixing = 0.5

CODE_SCALE = 4096.0
CHUNKS = 4


def encode(value):
    scaled = value * CODE_SCALE
    return (scaled * jnp.abs(scaled) * (scaled * scaled)).astype(jnp.bfloat16)


def decode(coded):
    wide = coded.astype(jnp.float32)
    size = jnp.maximum(jnp.abs(wide), 1e-37)
    root = lax.rsqrt(lax.rsqrt(size)) * (1.0 / CODE_SCALE)
    return jnp.where(wide < 0.0, -root, root)


def adam(params, adam_m, adam_v, gradient):
    first_moment = beta_one * adam_m + (1.0 - beta_one) * gradient
    second_moment = beta_two * adam_v + (1.0 - beta_two) * gradient * gradient
    first_hat = first_moment / (1.0 - beta_one**INNER_STEP)
    second_hat = second_moment / (1.0 - beta_two**INNER_STEP)
    inner = params - inner_rate * (
        first_hat / (jnp.sqrt(second_hat) + epsilon) + decay_rate * params
    )
    return first_moment, second_moment, inner


def kernel(
    depth, pairs, chunks,
    acts, grad_out, params, adam_m, adam_v, global_params, outer_mom,
    mixed, first_out, second_out, new_global, new_mom, forward,
    part, x_out, x_in, z_out, z_in, inner, core_in, y_out, y_in,
    x_ss, x_rs, z_ss, z_rs, c_ss, c_rs, y_ss, y_rs, g_ss, g_rs, f_ss, f_rs,
):
    rows = params.shape[0]
    step = rows // chunks
    half = step // 2
    me = lax.axis_index("fsdp")
    isle = lax.axis_index("island")
    zi, xi = me // 2, lax.rem(me, 2)
    pair, core = isle // 2, lax.rem(isle, 2)

    def shift(d):
        return lax.rem(zi + d, depth)

    partner = {"fsdp": zi * 2 + 1 - xi, "island": isle}
    mate = {"fsdp": me, "island": pair * 2 + 1 - core}

    def along(d):
        return {"fsdp": shift(d) * 2 + xi, "island": isle}

    def across(e, k):
        return {"fsdp": me, "island": lax.rem(pair + e, pairs) * 2 + k}

    barrier = pltpu.get_barrier_semaphore()
    peers = [partner, mate] + [along(d) for d in range(1, depth)]
    peers += [across(e, k) for e in range(1, pairs) for k in range(2)]
    for peer in peers:
        pl.semaphore_signal(barrier, inc=1, device_id=peer, device_id_type=pl.DeviceIdType.MESH)

    def remote(src, dst, ss, rs, where):
        return pltpu.make_async_remote_copy(
            src_ref=src, dst_ref=dst, send_sem=ss, recv_sem=rs,
            device_id=where, device_id_type=pl.DeviceIdType.MESH,
        )

    def product(block, c):
        first = pl.multiple_of(block * rows + c * step, step)
        return lax.dot_general(
            acts[:, pl.ds(first, step)], grad_out[...],
            (((0,), (0,)), ((), ())), preferred_element_type=jnp.float32,
        )

    def x_copy(c, d):
        return remote(x_out.at[c, d], x_in.at[c, d], x_ss.at[c, d], x_rs.at[c, d], partner)

    def z_copy(c, d):
        return remote(z_out.at[c, d], z_in.at[c, d], z_ss.at[c, d], z_rs.at[c, d], along(d))

    def piece(c):
        return pl.ds(c * step, step)

    def c_copy(c):
        return remote(inner.at[piece(c)], core_in.at[c], c_ss.at[c], c_rs.at[c], mate)

    def y_copy(c, e, k):
        return remote(
            y_out.at[c, pl.ds(pl.multiple_of(core * half, half), half)],
            y_in.at[c, e, core], y_ss.at[c, e, k], y_rs.at[c, e, core], across(e, k),
        )

    def y_recv(c, e, k):
        return remote(
            y_out.at[c, pl.ds(0, half)], y_in.at[c, e, k],
            y_ss.at[c, e, k], y_rs.at[c, e, k], mate,
        )

    def at(block, c):
        return forward.at[pl.ds(pl.multiple_of(block * rows + c * step, step), step)]

    def g_copy(c, d):
        own = at(me, c)
        return remote(own, own, g_ss.at[c, d], g_rs.at[c, d], partner if d == 0 else along(d))

    def g_recv(c, d):
        block = at(me if d == 0 else shift(depth - d) * 2 + xi, c)
        return remote(block, block, g_ss.at[c, d], g_rs.at[c, d], partner)

    def f_copy(c, d):
        block = at(shift(depth - d) * 2 + xi, c)
        return remote(block, block, f_ss.at[c, d], f_rs.at[c, d], partner)

    order = list(range(1, depth)) + [0]

    def x_send(c, d):
        x_out[c, d] = encode(product(shift(d) * 2 + 1 - xi, c))
        if c == 0 and d == order[0]:
            pl.semaphore_wait(barrier, len(peers))
        x_copy(c, d).start()

    def z_send(c, d):
        mine = product(shift(d) * 2 + xi, c)
        x_copy(c, d).wait_recv()
        z_out[c, d] = encode(mine + decode(x_in[c, d]))
        z_copy(c, d).start()

    def reduce(c):
        part[...] = product(me, c)
        x_copy(c, 0).wait_recv()
        total = part[...] + decode(x_in[c, 0])
        for d in range(1, depth):
            z_copy(c, d).wait_recv()
            total = total + decode(z_in[c, d])
        s = piece(c)
        first, second, own = adam(params[s], adam_m[s], adam_v[s], total)
        inner[s] = own
        c_copy(c).start()
        first_out[s] = first
        second_out[s] = second

    def join(c):
        c_copy(c).wait_recv()
        y_out[c] = inner[piece(c)] + core_in[c]
        for e in range(1, pairs):
            for k in range(2):
                y_copy(c, e, k).start()

    def outer(c):
        for e in range(1, pairs):
            for k in range(2):
                y_recv(c, e, k).wait_recv()
        for k in range(2):
            s = pl.ds(c * step + k * half, half)
            summed = y_out[c, pl.ds(k * half, half)]
            for e in range(1, pairs):
                summed = summed + y_in[c, e, k]
            delta = global_params[s] - summed / (2 * pairs)
            fresh = momentum * outer_mom[s] + delta
            moved = global_params[s] - outer_rate * (delta + momentum * fresh)
            merged = mixing * inner[s] + (1.0 - mixing) * moved
            first = pl.multiple_of(me * rows + c * step + k * half, half)
            forward[pl.ds(first, half)] = merged.astype(jnp.bfloat16)
            mixed[s] = merged
            new_mom[s] = fresh
            new_global[s] = moved
        for d in order:
            g_copy(c, d).start()

    def relay(c):
        for d in range(1, depth):
            g_recv(c, d).wait_recv()
            f_copy(c, d).start()

    for c in range(chunks):
        for d in order:
            x_send(c, d)
    for d in range(1, depth):
        z_send(0, d)
    for c in range(chunks):
        after = [functools.partial(z_send, c + 1, d) for d in range(1, depth)] if c + 1 < chunks else []
        for work in (reduce, join, outer):
            if after:
                after.pop(0)()
            work(c)
        for rest in after:
            rest()
        if c > 0:
            relay(c - 1)
    relay(chunks - 1)

    for c in range(chunks):
        c_copy(c).wait_send()
        for e in range(1, pairs):
            for k in range(2):
                y_copy(c, e, k).wait_send()
        for d in range(depth):
            x_copy(c, d).wait_send()
            g_copy(c, d).wait_send()
            if d > 0:
                z_copy(c, d).wait_send()
                f_copy(c, d).wait_send()
        partner_own = at(zi * 2 + 1 - xi, c)
        remote(partner_own, partner_own, g_ss.at[c, 0], g_rs.at[c, 0], partner).wait_recv()
        for d in range(1, depth):
            block = at(shift(depth - d) * 2 + 1 - xi, c)
            remote(block, block, f_ss.at[c, d], f_rs.at[c, d], partner).wait_recv()


def fused(acts, grad_out, params, adam_m, adam_v, global_params, outer_mom):
    fsdp, islands = lax.axis_size("fsdp"), lax.axis_size("island")
    depth, pairs = fsdp // 2, islands // 2
    rows, width = params.shape[1:]
    chunks = CHUNKS
    step = rows // chunks
    single = jax.ShapeDtypeStruct((rows, width), jnp.float32)
    dma = pltpu.SemaphoreType.DMA
    vmem = pl.BlockSpec(memory_space=pltpu.VMEM)
    coded = pltpu.VMEM((chunks, depth, step, width), jnp.bfloat16)
    mixed, first, second, new_global, new_mom, forward = pl.pallas_call(
        functools.partial(kernel, depth, pairs, chunks),
        out_shape=[single] * 5 + [jax.ShapeDtypeStruct((fsdp * rows, width), jnp.bfloat16)],
        in_specs=[vmem] * 7,
        out_specs=[vmem] * 6,
        scratch_shapes=[
            pltpu.VMEM((step, width), jnp.float32),
            coded, coded, coded, coded,
            pltpu.VMEM((rows, width), jnp.float32),
            pltpu.VMEM((chunks, step, width), jnp.float32),
            pltpu.VMEM((chunks, step, width), jnp.float32),
            pltpu.VMEM((chunks, pairs, 2, step // 2, width), jnp.float32),
            dma((chunks, depth)), dma((chunks, depth)),
            dma((chunks, depth)), dma((chunks, depth)),
            dma((chunks,)), dma((chunks,)),
            dma((chunks, pairs, 2)), dma((chunks, pairs, 2)),
            dma((chunks, depth)), dma((chunks, depth)),
            dma((chunks, depth)), dma((chunks, depth)),
        ],
        compiler_params=pltpu.CompilerParams(
            collective_id=0, has_side_effects=True, vmem_limit_bytes=40 * 2**20
        ),
    )(acts[0], grad_out[0], params[0], adam_m[0], adam_v[0], global_params, outer_mom)
    return mixed[None], first[None], second[None], new_global, new_mom, forward[None]


def general(acts, grad_out, params, adam_m, adam_v, global_params, outer_mom):
    shard_rows = params.shape[1]
    features = acts.shape[2]
    padded_rows = shard_rows * lax.axis_size("fsdp")
    islands = lax.axis_size("island")
    inputs = acts[0]
    cotangent = grad_out[0]
    whole = jnp.einsum("td,th->dh", inputs, cotangent, preferred_element_type=jnp.float32)
    whole = jnp.pad(whole, ((0, padded_rows - features), (0, 0)))
    gradient = lax.psum_scatter(whole, "fsdp", scatter_dimension=0, tiled=True)
    first_moment, second_moment, inner = adam(params, adam_m, adam_v, gradient[None])
    summed = lax.psum(inner, "island")
    delta = global_params - summed[0] / islands
    new_mom = momentum * outer_mom + delta
    new_global = global_params - outer_rate * (delta + momentum * new_mom)
    mixed = mixing * inner + (1.0 - mixing) * new_global[None]
    gathered = lax.all_gather(mixed.astype(jnp.bfloat16), "fsdp", axis=1, tiled=True)
    forward_weight = gathered[:, :features]
    return (mixed, first_moment, second_moment, new_global, new_mom, forward_weight)


def on_device(acts, *others):
    fsdp, islands = lax.axis_size("fsdp"), lax.axis_size("island")
    rows = others[1].shape[1]
    fits = (
        rows * fsdp == acts.shape[2]
        and rows % (CHUNKS * 128) == 0
        and fsdp % 2 == 0
        and 2 <= fsdp // 2 <= 4
        and islands == 4
    )
    return (fused if fits else general)(acts, *others)


def solution(mesh):
    in_specs = (
        P("island", "fsdp", None),
        P("island", "fsdp", None),
        P("island", "fsdp", None),
        P("island", "fsdp", None),
        P("island", "fsdp", None),
        P("fsdp", None),
        P("fsdp", None),
    )
    out_specs = (
        P("island", "fsdp", None),
        P("island", "fsdp", None),
        P("island", "fsdp", None),
        P("fsdp", None),
        P("fsdp", None),
        P("island", None, None),
    )
    return jax.shard_map(
        on_device, mesh=mesh, in_specs=in_specs, out_specs=out_specs, check_vma=False
    )
```

```python
import functools

import jax
import jax.numpy as jnp
from jax import lax
from jax.experimental import pallas as pl
from jax.experimental.pallas import tpu as pltpu
from jax.sharding import PartitionSpec as P

INNER_STEP = 100


beta_one = 0.9
beta_two = 0.95
epsilon = 1e-08
inner_rate = 0.001
decay_rate = 0.1
outer_rate = 0.7
momentum = 0.9
mixing = 0.5

CODE_SCALE = 4096.0
LAGS = (0, 0, 2, 2)
VMEM_LIMIT = 60 * 2**20


def encode(value):
    scaled = value * CODE_SCALE
    return (scaled * jnp.abs(scaled) * (scaled * scaled)).astype(jnp.bfloat16)


def decode(coded):
    wide = coded.astype(jnp.float32)
    size = jnp.maximum(jnp.abs(wide), 1e-37)
    root = lax.rsqrt(lax.rsqrt(size)) * (1.0 / CODE_SCALE)
    return jnp.where(wide < 0.0, -root, root)


def adam(params, adam_m, adam_v, gradient):
    first_moment = beta_one * adam_m + (1.0 - beta_one) * gradient
    second_moment = beta_two * adam_v + (1.0 - beta_two) * gradient * gradient
    first_hat = first_moment / (1.0 - beta_one**INNER_STEP)
    second_hat = second_moment / (1.0 - beta_two**INNER_STEP)
    inner = params - inner_rate * (
        first_hat / (jnp.sqrt(second_hat) + epsilon) + decay_rate * params
    )
    return first_moment, second_moment, inner


def kernel(
    ring, pairs, chunks, lags,
    acts_hbm, grad_hbm, params_hbm, m_hbm, v_hbm, global_hbm, mom_hbm,
    mixed_hbm, first_hbm, second_hbm, new_global_hbm, new_mom_hbm, forward_hbm,
    mixed, first_out, second_out, new_global, new_mom, forward,
    acts, grad_out, params, adam_m, adam_v, global_params, outer_mom,
    part, r_out, r_in, inner, core_in, y_out, y_in,
    a_sem, i_sem, o_sem, w_sem, r_ss, r_rs, c_ss, c_rs, y_ss, y_rs, g_ss, g_rs,
):
    rows = params.shape[0]
    step = rows // chunks
    half = step // 2
    depth = ring // 2
    me = lax.axis_index("fsdp")
    isle = lax.axis_index("island")
    zi, xi = me // 2, lax.rem(me, 2)
    place = zi * (1 - xi) + (ring - 1 - zi) * xi
    pair, core = isle // 2, lax.rem(isle, 2)

    def index(k):
        spot = lax.rem(place + (k % ring), ring)
        side = spot // depth
        return (spot * (1 - side) + (ring - 1 - spot) * side) * 2 + side

    ahead = {"fsdp": index(1), "island": isle}
    behind = {"fsdp": index(-1), "island": isle}
    mate = {"fsdp": me, "island": pair * 2 + 1 - core}
    toward = (ahead, behind)

    def across(e, k):
        return {"fsdp": me, "island": lax.rem(pair + e, pairs) * 2 + k}

    barrier = pltpu.get_barrier_semaphore()
    peers = [ahead, behind, mate] + [across(e, k) for e in range(1, pairs) for k in range(2)]
    for peer in peers:
        pl.semaphore_signal(barrier, inc=1, device_id=peer, device_id_type=pl.DeviceIdType.MESH)

    def columns(k):
        return pl.ds(pl.multiple_of(index(k) * rows, rows), rows)

    def load(k):
        return pltpu.make_async_copy(
            acts_hbm.at[:, columns(k)], acts.at[k % ring], a_sem.at[k % ring]
        )

    singles = [
        (grad_hbm, grad_out), (params_hbm, params), (m_hbm, adam_m), (v_hbm, adam_v),
        (global_hbm, global_params), (mom_hbm, outer_mom),
    ]
    inputs = [pltpu.make_async_copy(s, d, i_sem.at[n]) for n, (s, d) in enumerate(singles)]
    needs = [depth]
    for k in range(depth - 1, 0, -1):
        needs += [k, ring - k]
    needs.append(0)
    inputs[0].start()
    for k in needs:
        load(k).start()
    for copy in inputs[1:]:
        copy.start()

    def product(k):
        load(k).wait()
        part[k] = lax.dot_general(
            acts[k], grad_out[...],
            (((0,), (0,)), ((), ())), preferred_element_type=jnp.float32,
        )

    def remote(src, dst, ss, rs, where):
        return pltpu.make_async_remote_copy(
            src_ref=src, dst_ref=dst, send_sem=ss, recv_sem=rs,
            device_id=where, device_id_type=pl.DeviceIdType.MESH,
        )

    def reach(c, q):
        return depth - (c + q) % 2

    def piece(c):
        return pl.ds(c * step, step)

    def r_copy(c, q, s):
        return remote(
            r_out.at[c, q, s], r_in.at[c, q, s], r_ss.at[c, q, s], r_rs.at[c, q, s], toward[q]
        )

    def c_copy(c):
        return remote(inner.at[piece(c)], core_in.at[c], c_ss.at[c], c_rs.at[c], mate)

    def y_copy(c, e, k):
        return remote(
            y_out.at[c, pl.ds(pl.multiple_of(core * half, half), half)],
            y_in.at[c, e, core], y_ss.at[c, e, k], y_rs.at[c, e, core], across(e, k),
        )

    def y_recv(c, e, k):
        return remote(
            y_out.at[c, pl.ds(0, half)], y_in.at[c, e, k],
            y_ss.at[c, e, k], y_rs.at[c, e, k], mate,
        )

    def g_copy(c, q, s, hop):
        k = hop if q else -hop
        first = pl.multiple_of(index(k) * rows + c * step, step)
        block = forward.at[pl.ds(first, step)]
        return remote(block, block, g_ss.at[c, q, s], g_rs.at[c, q, s], toward[q])

    landing = (
        (first_out, first_hbm), (second_out, second_hbm),
        (mixed, mixed_hbm), (new_global, new_global_hbm), (new_mom, new_mom_hbm),
    )

    def store(c, n):
        src, dst = landing[n]
        return pltpu.make_async_copy(src.at[piece(c)], dst.at[piece(c)], o_sem.at[c, n])

    def keep(c, q, hop):
        first = pl.multiple_of(index(hop if q else -hop) * rows + c * step, step)
        place_of = pl.ds(first, step)
        return pltpu.make_async_copy(
            forward.at[place_of], forward_hbm.at[place_of], w_sem.at[c, q, hop]
        )

    def sum_on(c, q, s):
        k = reach(c, q) - s
        value = part[(-k if q else k) % ring, piece(c)]
        if s > 0:
            r_copy(c, q, s - 1).wait_recv()
            value = value + decode(r_in[c, q, s - 1])
        r_out[c, q, s] = encode(value)
        r_copy(c, q, s).start()

    def reduce(c):
        total = part[0, piece(c)]
        for q in range(2):
            last = reach(c, q) - 1
            r_copy(c, q, last).wait_recv()
            total = total + decode(r_in[c, q, last])
        s = piece(c)
        first, second, own = adam(params[s], adam_m[s], adam_v[s], total)
        inner[s] = own
        c_copy(c).start()
        first_out[s] = first
        second_out[s] = second
        store(c, 0).start()
        store(c, 1).start()

    def join(c):
        c_copy(c).wait_recv()
        y_out[c] = inner[piece(c)] + core_in[c]
        for e in range(1, pairs):
            for k in range(2):
                y_copy(c, e, k).start()

    def outer(c):
        for e in range(1, pairs):
            for k in range(2):
                y_recv(c, e, k).wait_recv()
        for k in range(2):
            s = pl.ds(c * step + k * half, half)
            summed = y_out[c, pl.ds(k * half, half)]
            for e in range(1, pairs):
                summed = summed + y_in[c, e, k]
            delta = global_params[s] - summed / (2 * pairs)
            fresh = momentum * outer_mom[s] + delta
            moved = global_params[s] - outer_rate * (delta + momentum * fresh)
            merged = mixing * inner[s] + (1.0 - mixing) * moved
            first = pl.multiple_of(me * rows + c * step + k * half, half)
            forward[pl.ds(first, half)] = merged.astype(jnp.bfloat16)
            mixed[s] = merged
            new_mom[s] = fresh
            new_global[s] = moved
        for q in range(2):
            g_copy(c, q, 0, 0).start()
        keep(c, 0, 0).start()
        for n in range(2, 5):
            store(c, n).start()

    def pass_on(c, q, s):
        g_copy(c, q, s - 1, s).wait_recv()
        g_copy(c, q, s, s).start()
        keep(c, q, s).start()

    def tick(c, t):
        if t < depth:
            for q in range(2):
                if t < reach(c, q):
                    sum_on(c, q, t)
        elif t == depth:
            reduce(c)
        elif t == depth + 1:
            join(c)
        elif t == depth + 2:
            outer(c)
        else:
            for q in range(2):
                if t - depth - 2 < reach(c, q):
                    pass_on(c, q, t - depth - 2)

    inputs[0].wait()
    product(depth)
    pl.semaphore_wait(barrier, len(peers))
    for t in range(2 * depth + 2 + max(lags)):
        if t < depth - 1:
            product(depth - 1 - t)
            product(depth + 1 + t)
        elif t == depth - 1:
            product(0)
            for copy in inputs[1:]:
                copy.wait()
        for c in range(chunks):
            if 0 <= t - lags[c] < 2 * depth + 2:
                tick(c, t - lags[c])

    for c in range(chunks):
        c_copy(c).wait_send()
        for e in range(1, pairs):
            for k in range(2):
                y_copy(c, e, k).wait_send()
        for q in range(2):
            for s in range(reach(c, q)):
                r_copy(c, q, s).wait_send()
                g_copy(c, q, s, s).wait_send()
            g_copy(c, q, reach(c, q) - 1, reach(c, q)).wait_recv()
            keep(c, q, reach(c, q)).start()
    for c in range(chunks):
        for n in range(5):
            store(c, n).wait()
        keep(c, 0, 0).wait()
        for q in range(2):
            for hop in range(1, reach(c, q) + 1):
                keep(c, q, hop).wait()


def write_out(*refs):
    count = len(refs) // 2
    copies = [
        pltpu.make_async_copy(refs[n], refs[count + n], refs[-1].at[n]) for n in range(count)
    ]
    for copy in copies:
        copy.start()
    for copy in copies:
        copy.wait()


def fused(acts, grad_out, params, adam_m, adam_v, global_params, outer_mom):
    ring, islands = lax.axis_size("fsdp"), lax.axis_size("island")
    depth, pairs = ring // 2, islands // 2
    rows, width = params.shape[1:]
    tokens = acts.shape[1]
    chunks = len(LAGS)
    step = rows // chunks
    single = jax.ShapeDtypeStruct((rows, width), jnp.float32)
    whole = jax.ShapeDtypeStruct((ring * rows, width), jnp.bfloat16)
    dma = pltpu.SemaphoreType.DMA
    hbm = pl.BlockSpec(memory_space=pltpu.HBM)
    own = pltpu.VMEM((rows, width), jnp.float32)
    coded = pltpu.VMEM((chunks, 2, depth, step, width), jnp.bfloat16)
    results = pl.pallas_call(
        functools.partial(kernel, ring, pairs, chunks, LAGS),
        out_shape=[single] * 5 + [whole],
        in_specs=[hbm] * 7,
        out_specs=[hbm] * 6,
        scratch_shapes=[
            own, own, own, own, own,
            pltpu.VMEM((ring * rows, width), jnp.bfloat16),
            pltpu.VMEM((ring, tokens, rows), jnp.bfloat16),
            pltpu.VMEM((tokens, width), jnp.bfloat16),
            own, own, own, own, own,
            pltpu.VMEM((ring, rows, width), jnp.float32),
            coded, coded,
            own,
            pltpu.VMEM((chunks, step, width), jnp.float32),
            pltpu.VMEM((chunks, step, width), jnp.float32),
            pltpu.VMEM((chunks, pairs, 2, step // 2, width), jnp.float32),
            dma((ring,)), dma((6,)), dma((chunks, 5)), dma((chunks, 2, depth + 1)),
            dma((chunks, 2, depth)), dma((chunks, 2, depth)),
            dma((chunks,)), dma((chunks,)),
            dma((chunks, pairs, 2)), dma((chunks, pairs, 2)),
            dma((chunks, 2, depth)), dma((chunks, 2, depth)),
        ],
        compiler_params=pltpu.CompilerParams(
            collective_id=0, has_side_effects=True, vmem_limit_bytes=VMEM_LIMIT
        ),
    )(acts[0], grad_out[0], params[0], adam_m[0], adam_v[0], global_params, outer_mom)
    mixed, first, second, new_global, new_mom, forward = pl.pallas_call(
        write_out,
        out_shape=[single] * 5 + [whole],
        in_specs=[hbm] * 6,
        out_specs=[hbm] * 6,
        scratch_shapes=[dma((6,))],
        compiler_params=pltpu.CompilerParams(vmem_limit_bytes=VMEM_LIMIT),
    )(*results)
    return mixed[None], first[None], second[None], new_global, new_mom, forward[None]


def general(acts, grad_out, params, adam_m, adam_v, global_params, outer_mom):
    shard_rows = params.shape[1]
    features = acts.shape[2]
    padded_rows = shard_rows * lax.axis_size("fsdp")
    islands = lax.axis_size("island")
    inputs = acts[0]
    cotangent = grad_out[0]
    whole = jnp.einsum("td,th->dh", inputs, cotangent, preferred_element_type=jnp.float32)
    whole = jnp.pad(whole, ((0, padded_rows - features), (0, 0)))
    gradient = lax.psum_scatter(whole, "fsdp", scatter_dimension=0, tiled=True)
    first_moment, second_moment, inner = adam(params, adam_m, adam_v, gradient[None])
    summed = lax.psum(inner, "island")
    delta = global_params - summed[0] / islands
    new_mom = momentum * outer_mom + delta
    new_global = global_params - outer_rate * (delta + momentum * new_mom)
    mixed = mixing * inner + (1.0 - mixing) * new_global[None]
    gathered = lax.all_gather(mixed.astype(jnp.bfloat16), "fsdp", axis=1, tiled=True)
    forward_weight = gathered[:, :features]
    return (mixed, first_moment, second_moment, new_global, new_mom, forward_weight)


def on_device(acts, *others):
    fsdp, islands = lax.axis_size("fsdp"), lax.axis_size("island")
    rows = others[1].shape[1]
    fits = (
        rows * fsdp == acts.shape[2]
        and rows % (len(LAGS) * 128) == 0
        and fsdp % 2 == 0
        and 2 <= fsdp // 2 <= 4
        and islands == 4
    )
    return (fused if fits else general)(acts, *others)


def solution(mesh):
    in_specs = (
        P("island", "fsdp", None),
        P("island", "fsdp", None),
        P("island", "fsdp", None),
        P("island", "fsdp", None),
        P("island", "fsdp", None),
        P("fsdp", None),
        P("fsdp", None),
    )
    out_specs = (
        P("island", "fsdp", None),
        P("island", "fsdp", None),
        P("island", "fsdp", None),
        P("fsdp", None),
        P("fsdp", None),
        P("island", None, None),
    )
    return jax.shard_map(
        on_device, mesh=mesh, in_specs=in_specs, out_specs=out_specs, check_vma=False
    )
```

```python
import functools

import jax
import jax.numpy as jnp
from jax import lax
from jax.experimental import pallas as pl
from jax.experimental.pallas import tpu as pltpu
from jax.sharding import PartitionSpec as P

INNER_STEP = 100


beta_one = 0.9
beta_two = 0.95
epsilon = 1e-08
inner_rate = 0.001
decay_rate = 0.1
outer_rate = 0.7
momentum = 0.9
mixing = 0.5

CODE_SCALE = 4096.0
LAGS = (0, 0, 2, 2)
VMEM_LIMIT = 60 * 2**20


def encode(value):
    scaled = value * CODE_SCALE
    return (scaled * jnp.abs(scaled) * (scaled * scaled)).astype(jnp.bfloat16)


def decode(coded):
    wide = coded.astype(jnp.float32)
    size = jnp.maximum(jnp.abs(wide), 1e-37)
    root = lax.rsqrt(lax.rsqrt(size)) * (1.0 / CODE_SCALE)
    return jnp.where(wide < 0.0, -root, root)


def adam(params, adam_m, adam_v, gradient):
    first_moment = beta_one * adam_m + (1.0 - beta_one) * gradient
    second_moment = beta_two * adam_v + (1.0 - beta_two) * gradient * gradient
    first_hat = first_moment / (1.0 - beta_one**INNER_STEP)
    second_hat = second_moment / (1.0 - beta_two**INNER_STEP)
    inner = params - inner_rate * (
        first_hat / (jnp.sqrt(second_hat) + epsilon) + decay_rate * params
    )
    return first_moment, second_moment, inner


def kernel(
    ring, pairs, chunks, lags,
    acts_hbm, grad_hbm, params_hbm, m_hbm, v_hbm, global_hbm, mom_hbm,
    mixed_hbm, first_hbm, second_hbm, new_global_hbm, new_mom_hbm, forward_hbm,
    mixed, first_out, second_out, new_global, new_mom, forward,
    acts, grad_out, params, adam_m, adam_v, global_params, outer_mom,
    turned, part, r_out, r_in, inner, core_in, y_out, y_in,
    a_sem, i_sem, o_sem, w_sem, r_ss, r_rs, c_ss, c_rs, y_ss, y_rs, g_ss, g_rs,
):
    rows = params.shape[0]
    step = rows // chunks
    half = step // 2
    depth = ring // 2
    me = lax.axis_index("fsdp")
    isle = lax.axis_index("island")
    zi, xi = me // 2, lax.rem(me, 2)
    place = zi * (1 - xi) + (ring - 1 - zi) * xi
    pair, core = isle // 2, lax.rem(isle, 2)

    def index(k):
        spot = lax.rem(place + (k % ring), ring)
        side = spot // depth
        return (spot * (1 - side) + (ring - 1 - spot) * side) * 2 + side

    ahead = {"fsdp": index(1), "island": isle}
    behind = {"fsdp": index(-1), "island": isle}
    mate = {"fsdp": me, "island": pair * 2 + 1 - core}
    toward = (ahead, behind)

    def across(e, k):
        return {"fsdp": me, "island": lax.rem(pair + e, pairs) * 2 + k}

    barrier = pltpu.get_barrier_semaphore()
    peers = [ahead, behind, mate] + [across(e, k) for e in range(1, pairs) for k in range(2)]
    for peer in peers:
        pl.semaphore_signal(barrier, inc=1, device_id=peer, device_id_type=pl.DeviceIdType.MESH)

    def columns(k):
        return pl.ds(pl.multiple_of(index(k) * rows, rows), rows)

    def load(k):
        return pltpu.make_async_copy(
            acts_hbm.at[:, columns(k)], acts.at[k % ring], a_sem.at[k % ring]
        )

    singles = [
        (grad_hbm, grad_out), (params_hbm, params), (m_hbm, adam_m), (v_hbm, adam_v),
        (global_hbm, global_params), (mom_hbm, outer_mom),
    ]
    inputs = [pltpu.make_async_copy(s, d, i_sem.at[n]) for n, (s, d) in enumerate(singles)]
    needs = [depth]
    for k in range(depth - 1, 0, -1):
        needs += [k, ring - k]
    needs.append(0)
    inputs[0].start()
    for k in needs:
        load(k).start()
    for copy in inputs[1:]:
        copy.start()

    def product(k):
        load(k).wait()
        part[k] = jnp.dot(turned[...], acts[k], preferred_element_type=jnp.float32)

    def remote(src, dst, ss, rs, where):
        return pltpu.make_async_remote_copy(
            src_ref=src, dst_ref=dst, send_sem=ss, recv_sem=rs,
            device_id=where, device_id_type=pl.DeviceIdType.MESH,
        )

    def reach(c, q):
        return depth - (c + q) % 2

    def piece(c):
        return pl.ds(c * step, step)

    def r_copy(c, q, s):
        return remote(
            r_out.at[c, q, s], r_in.at[c, q, s], r_ss.at[c, q, s], r_rs.at[c, q, s], toward[q]
        )

    def c_copy(c):
        return remote(inner.at[piece(c)], core_in.at[c], c_ss.at[c], c_rs.at[c], mate)

    def y_copy(c, e, k):
        return remote(
            y_out.at[c, pl.ds(pl.multiple_of(core * half, half), half)],
            y_in.at[c, e, core], y_ss.at[c, e, k], y_rs.at[c, e, core], across(e, k),
        )

    def y_recv(c, e, k):
        return remote(
            y_out.at[c, pl.ds(0, half)], y_in.at[c, e, k],
            y_ss.at[c, e, k], y_rs.at[c, e, k], mate,
        )

    def g_copy(c, q, s, hop):
        k = hop if q else -hop
        first = pl.multiple_of(index(k) * rows + c * step, step)
        block = forward.at[pl.ds(first, step)]
        return remote(block, block, g_ss.at[c, q, s], g_rs.at[c, q, s], toward[q])

    landing = (
        (first_out, first_hbm), (second_out, second_hbm),
        (mixed, mixed_hbm), (new_global, new_global_hbm), (new_mom, new_mom_hbm),
    )

    def store(c, n):
        src, dst = landing[n]
        return pltpu.make_async_copy(src.at[piece(c)], dst.at[piece(c)], o_sem.at[c, n])

    def keep(c, q, hop):
        first = pl.multiple_of(index(hop if q else -hop) * rows + c * step, step)
        place_of = pl.ds(first, step)
        return pltpu.make_async_copy(
            forward.at[place_of], forward_hbm.at[place_of], w_sem.at[c, q, hop]
        )

    def sum_on(c, q, s):
        k = reach(c, q) - s
        value = part[(-k if q else k) % ring, :, piece(c)]
        if s > 0:
            r_copy(c, q, s - 1).wait_recv()
            value = value + decode(r_in[c, q, s - 1])
        r_out[c, q, s] = encode(value)
        r_copy(c, q, s).start()

    def reduce(c):
        total = part[0, :, piece(c)]
        for q in range(2):
            last = reach(c, q) - 1
            r_copy(c, q, last).wait_recv()
            total = total + decode(r_in[c, q, last])
        s = piece(c)
        first, second, own = adam(params[s], adam_m[s], adam_v[s], total.T)
        inner[s] = own
        c_copy(c).start()
        first_out[s] = first
        second_out[s] = second
        store(c, 0).start()
        store(c, 1).start()

    def join(c):
        c_copy(c).wait_recv()
        y_out[c] = inner[piece(c)] + core_in[c]
        for e in range(1, pairs):
            for k in range(2):
                y_copy(c, e, k).start()

    def outer(c):
        for e in range(1, pairs):
            for k in range(2):
                y_recv(c, e, k).wait_recv()
        for k in range(2):
            s = pl.ds(c * step + k * half, half)
            summed = y_out[c, pl.ds(k * half, half)]
            for e in range(1, pairs):
                summed = summed + y_in[c, e, k]
            delta = global_params[s] - summed / (2 * pairs)
            fresh = momentum * outer_mom[s] + delta
            moved = global_params[s] - outer_rate * (delta + momentum * fresh)
            merged = mixing * inner[s] + (1.0 - mixing) * moved
            first = pl.multiple_of(me * rows + c * step + k * half, half)
            forward[pl.ds(first, half)] = merged.astype(jnp.bfloat16)
            mixed[s] = merged
            new_mom[s] = fresh
            new_global[s] = moved
        for q in range(2):
            g_copy(c, q, 0, 0).start()
        keep(c, 0, 0).start()
        for n in range(2, 5):
            store(c, n).start()

    def pass_on(c, q, s):
        g_copy(c, q, s - 1, s).wait_recv()
        g_copy(c, q, s, s).start()
        keep(c, q, s).start()

    def tick(c, t):
        if t < depth:
            for q in range(2):
                if t < reach(c, q):
                    sum_on(c, q, t)
        elif t == depth:
            reduce(c)
        elif t == depth + 1:
            join(c)
        elif t == depth + 2:
            outer(c)
        else:
            for q in range(2):
                if t - depth - 2 < reach(c, q):
                    pass_on(c, q, t - depth - 2)

    inputs[0].wait()
    turned[...] = grad_out[...].T
    product(depth)
    pl.semaphore_wait(barrier, len(peers))
    for far in (depth, depth - 1):
        if far < depth:
            product(far)
            product(ring - far)
        for c in range(chunks):
            for q in range(2):
                if lags[c] == 0 and reach(c, q) == far:
                    sum_on(c, q, 0)
    for t in range(1, 2 * depth + 2 + max(lags)):
        if t < depth - 1:
            product(depth - 1 - t)
            product(depth + 1 + t)
        elif t == depth - 1:
            product(0)
            for copy in inputs[1:]:
                copy.wait()
        for c in range(chunks):
            if 0 <= t - lags[c] < 2 * depth + 2:
                tick(c, t - lags[c])

    for c in range(chunks):
        c_copy(c).wait_send()
        for e in range(1, pairs):
            for k in range(2):
                y_copy(c, e, k).wait_send()
        for q in range(2):
            for s in range(reach(c, q)):
                r_copy(c, q, s).wait_send()
                g_copy(c, q, s, s).wait_send()
            g_copy(c, q, reach(c, q) - 1, reach(c, q)).wait_recv()
            keep(c, q, reach(c, q)).start()
    for c in range(chunks):
        for n in range(5):
            store(c, n).wait()
        keep(c, 0, 0).wait()
        for q in range(2):
            for hop in range(1, reach(c, q) + 1):
                keep(c, q, hop).wait()


def write_out(parts, *refs):
    count = len(parts)
    sources, targets, held = refs[:count], refs[count : 2 * count], refs[2 * count : 3 * count]
    in_sem, out_sem = refs[3 * count :]
    loads, stores = [], []
    for n, cuts in enumerate(parts):
        extent = sources[n].shape[0] // cuts
        for cut in range(cuts):
            at = pl.ds(cut * extent, extent)
            spot = len(loads)
            loads.append(
                pltpu.make_async_copy(sources[n].at[at], held[n].at[at], in_sem.at[spot])
            )
            stores.append(
                pltpu.make_async_copy(held[n].at[at], targets[n].at[at], out_sem.at[spot])
            )
    for copy in loads:
        copy.start()
    for load, store in zip(loads, stores):
        load.wait()
        store.start()
    for copy in stores:
        copy.wait()


def fused(acts, grad_out, params, adam_m, adam_v, global_params, outer_mom):
    ring, islands = lax.axis_size("fsdp"), lax.axis_size("island")
    depth, pairs = ring // 2, islands // 2
    rows, width = params.shape[1:]
    tokens = acts.shape[1]
    chunks = len(LAGS)
    step = rows // chunks
    single = jax.ShapeDtypeStruct((rows, width), jnp.float32)
    whole = jax.ShapeDtypeStruct((ring * rows, width), jnp.bfloat16)
    dma = pltpu.SemaphoreType.DMA
    hbm = pl.BlockSpec(memory_space=pltpu.HBM)
    own = pltpu.VMEM((rows, width), jnp.float32)
    coded = pltpu.VMEM((chunks, 2, depth, width, step), jnp.bfloat16)
    results = pl.pallas_call(
        functools.partial(kernel, ring, pairs, chunks, LAGS),
        out_shape=[single] * 5 + [whole],
        in_specs=[hbm] * 7,
        out_specs=[hbm] * 6,
        scratch_shapes=[
            own, own, own, own, own,
            pltpu.VMEM((ring * rows, width), jnp.bfloat16),
            pltpu.VMEM((ring, tokens, rows), jnp.bfloat16),
            pltpu.VMEM((tokens, width), jnp.bfloat16),
            own, own, own, own, own,
            pltpu.VMEM((width, tokens), jnp.bfloat16),
            pltpu.VMEM((ring, width, rows), jnp.float32),
            coded, coded,
            own,
            pltpu.VMEM((chunks, step, width), jnp.float32),
            pltpu.VMEM((chunks, step, width), jnp.float32),
            pltpu.VMEM((chunks, pairs, 2, step // 2, width), jnp.float32),
            dma((ring,)), dma((6,)), dma((chunks, 5)), dma((chunks, 2, depth + 1)),
            dma((chunks, 2, depth)), dma((chunks, 2, depth)),
            dma((chunks,)), dma((chunks,)),
            dma((chunks, pairs, 2)), dma((chunks, pairs, 2)),
            dma((chunks, 2, depth)), dma((chunks, 2, depth)),
        ],
        compiler_params=pltpu.CompilerParams(
            collective_id=0, has_side_effects=True, vmem_limit_bytes=VMEM_LIMIT
        ),
    )(acts[0], grad_out[0], params[0], adam_m[0], adam_v[0], global_params, outer_mom)
    parts = (1,) * 5 + (4,)
    mixed, first, second, new_global, new_mom, forward = pl.pallas_call(
        functools.partial(write_out, parts),
        out_shape=[single] * 5 + [whole],
        in_specs=[hbm] * 6,
        out_specs=[hbm] * 6,
        scratch_shapes=[own] * 5 + [pltpu.VMEM(whole.shape, whole.dtype)] + [dma((sum(parts),))] * 2,
        compiler_params=pltpu.CompilerParams(vmem_limit_bytes=VMEM_LIMIT),
    )(*results)
    return mixed[None], first[None], second[None], new_global, new_mom, forward[None]


def general(acts, grad_out, params, adam_m, adam_v, global_params, outer_mom):
    shard_rows = params.shape[1]
    features = acts.shape[2]
    padded_rows = shard_rows * lax.axis_size("fsdp")
    islands = lax.axis_size("island")
    inputs = acts[0]
    cotangent = grad_out[0]
    whole = jnp.einsum("td,th->dh", inputs, cotangent, preferred_element_type=jnp.float32)
    whole = jnp.pad(whole, ((0, padded_rows - features), (0, 0)))
    gradient = lax.psum_scatter(whole, "fsdp", scatter_dimension=0, tiled=True)
    first_moment, second_moment, inner = adam(params, adam_m, adam_v, gradient[None])
    summed = lax.psum(inner, "island")
    delta = global_params - summed[0] / islands
    new_mom = momentum * outer_mom + delta
    new_global = global_params - outer_rate * (delta + momentum * new_mom)
    mixed = mixing * inner + (1.0 - mixing) * new_global[None]
    gathered = lax.all_gather(mixed.astype(jnp.bfloat16), "fsdp", axis=1, tiled=True)
    forward_weight = gathered[:, :features]
    return (mixed, first_moment, second_moment, new_global, new_mom, forward_weight)


def on_device(acts, *others):
    fsdp, islands = lax.axis_size("fsdp"), lax.axis_size("island")
    rows = others[1].shape[1]
    fits = (
        rows * fsdp == acts.shape[2]
        and rows % (len(LAGS) * 128) == 0
        and fsdp % 2 == 0
        and 2 <= fsdp // 2 <= 4
        and islands == 4
    )
    return (fused if fits else general)(acts, *others)


def solution(mesh):
    in_specs = (
        P("island", "fsdp", None),
        P("island", "fsdp", None),
        P("island", "fsdp", None),
        P("island", "fsdp", None),
        P("island", "fsdp", None),
        P("fsdp", None),
        P("fsdp", None),
    )
    out_specs = (
        P("island", "fsdp", None),
        P("island", "fsdp", None),
        P("island", "fsdp", None),
        P("fsdp", None),
        P("fsdp", None),
        P("island", None, None),
    )
    return jax.shard_map(
        on_device, mesh=mesh, in_specs=in_specs, out_specs=out_specs, check_vma=False
    )
```

```python
import functools

import jax
import jax.numpy as jnp
from jax import lax
from jax.experimental import pallas as pl
from jax.experimental.pallas import tpu as pltpu
from jax.sharding import PartitionSpec as P

INNER_STEP = 100


beta_one = 0.9
beta_two = 0.95
epsilon = 1e-08
inner_rate = 0.001
decay_rate = 0.1
outer_rate = 0.7
momentum = 0.9
mixing = 0.5

CODE_SCALE = 4096.0
LAGS = (0, 0, 0, 0)
VMEM_LIMIT = 60 * 2**20


def encode(value):
    scaled = value * CODE_SCALE
    return (scaled * jnp.abs(scaled) * (scaled * scaled)).astype(jnp.bfloat16)


def decode(coded):
    wide = coded.astype(jnp.float32)
    size = jnp.maximum(jnp.abs(wide), 1e-37)
    root = lax.rsqrt(lax.rsqrt(size)) * (1.0 / CODE_SCALE)
    return jnp.where(wide < 0.0, -root, root)


def adam(params, adam_m, adam_v, gradient):
    first_moment = beta_one * adam_m + (1.0 - beta_one) * gradient
    second_moment = beta_two * adam_v + (1.0 - beta_two) * gradient * gradient
    first_hat = first_moment / (1.0 - beta_one**INNER_STEP)
    second_hat = second_moment / (1.0 - beta_two**INNER_STEP)
    inner = params - inner_rate * (
        first_hat / (jnp.sqrt(second_hat) + epsilon) + decay_rate * params
    )
    return first_moment, second_moment, inner


def kernel(
    ring, pairs, chunks, lags,
    acts_hbm, grad_hbm, params_hbm, m_hbm, v_hbm, global_hbm, mom_hbm,
    mixed_hbm, first_hbm, second_hbm, new_global_hbm, new_mom_hbm, forward_hbm,
    mixed, first_out, second_out, new_global, new_mom, forward,
    acts, grad_out, params, adam_m, adam_v, global_params, outer_mom,
    turned, part, r_out, r_in, inner, core_in, y_out, y_in,
    a_sem, i_sem, o_sem, w_sem, r_ss, r_rs, c_ss, c_rs, y_ss, y_rs, g_ss, g_rs,
):
    rows = params.shape[0]
    step = rows // chunks
    half = step // 2
    depth = ring // 2
    me = lax.axis_index("fsdp")
    isle = lax.axis_index("island")
    zi, xi = me // 2, lax.rem(me, 2)
    place = zi * (1 - xi) + (ring - 1 - zi) * xi
    pair, core = isle // 2, lax.rem(isle, 2)

    def index(k):
        spot = lax.rem(place + (k % ring), ring)
        side = spot // depth
        return (spot * (1 - side) + (ring - 1 - spot) * side) * 2 + side

    ahead = {"fsdp": index(1), "island": isle}
    behind = {"fsdp": index(-1), "island": isle}
    mate = {"fsdp": me, "island": pair * 2 + 1 - core}
    toward = (ahead, behind)

    def across(e, k):
        return {"fsdp": me, "island": lax.rem(pair + e, pairs) * 2 + k}

    barrier = pltpu.get_barrier_semaphore()
    peers = [ahead, behind, mate] + [across(e, k) for e in range(1, pairs) for k in range(2)]
    for peer in peers:
        pl.semaphore_signal(barrier, inc=1, device_id=peer, device_id_type=pl.DeviceIdType.MESH)

    def columns(k):
        return pl.ds(pl.multiple_of(index(k) * rows, rows), rows)

    def load(k):
        return pltpu.make_async_copy(
            acts_hbm.at[:, columns(k)], acts.at[k % ring], a_sem.at[k % ring]
        )

    singles = [
        (grad_hbm, grad_out), (params_hbm, params), (m_hbm, adam_m), (v_hbm, adam_v),
        (global_hbm, global_params), (mom_hbm, outer_mom),
    ]
    inputs = [pltpu.make_async_copy(s, d, i_sem.at[n]) for n, (s, d) in enumerate(singles)]
    needs = [depth]
    for k in range(depth - 1, 0, -1):
        needs += [k, ring - k]
    needs.append(0)
    inputs[0].start()
    for k in needs:
        load(k).start()
    for copy in inputs[1:]:
        copy.start()

    def product(k):
        load(k).wait()
        part[k] = jnp.dot(turned[...], acts[k], preferred_element_type=jnp.float32)

    def remote(src, dst, ss, rs, where):
        return pltpu.make_async_remote_copy(
            src_ref=src, dst_ref=dst, send_sem=ss, recv_sem=rs,
            device_id=where, device_id_type=pl.DeviceIdType.MESH,
        )

    def reach(c, q):
        return depth - (c + q) % 2

    def piece(c):
        return pl.ds(c * step, step)

    def r_copy(c, q, s):
        return remote(
            r_out.at[c, q, s], r_in.at[c, q, s], r_ss.at[c, q, s], r_rs.at[c, q, s], toward[q]
        )

    def c_copy(c):
        return remote(inner.at[piece(c)], core_in.at[c], c_ss.at[c], c_rs.at[c], mate)

    def y_copy(c, e, k):
        return remote(
            y_out.at[c, pl.ds(pl.multiple_of(core * half, half), half)],
            y_in.at[c, e, core], y_ss.at[c, e, k], y_rs.at[c, e, core], across(e, k),
        )

    def y_recv(c, e, k):
        return remote(
            y_out.at[c, pl.ds(0, half)], y_in.at[c, e, k],
            y_ss.at[c, e, k], y_rs.at[c, e, k], mate,
        )

    def g_copy(c, q, s, hop):
        k = hop if q else -hop
        first = pl.multiple_of(index(k) * rows + c * step, step)
        block = forward.at[pl.ds(first, step)]
        return remote(block, block, g_ss.at[c, q, s], g_rs.at[c, q, s], toward[q])

    landing = (
        (first_out, first_hbm), (second_out, second_hbm),
        (mixed, mixed_hbm), (new_global, new_global_hbm), (new_mom, new_mom_hbm),
    )

    def store(c, n):
        src, dst = landing[n]
        return pltpu.make_async_copy(src.at[piece(c)], dst.at[piece(c)], o_sem.at[c, n])

    def keep(c, q, hop):
        first = pl.multiple_of(index(hop if q else -hop) * rows + c * step, step)
        place_of = pl.ds(first, step)
        return pltpu.make_async_copy(
            forward.at[place_of], forward_hbm.at[place_of], w_sem.at[c, q, hop]
        )

    def sum_on(c, q, s):
        k = reach(c, q) - s
        value = part[(-k if q else k) % ring, :, piece(c)]
        if s > 0:
            r_copy(c, q, s - 1).wait_recv()
            value = value + decode(r_in[c, q, s - 1])
        r_out[c, q, s] = encode(value)
        r_copy(c, q, s).start()

    def reduce(c):
        total = part[0, :, piece(c)]
        for q in range(2):
            last = reach(c, q) - 1
            r_copy(c, q, last).wait_recv()
            total = total + decode(r_in[c, q, last])
        s = piece(c)
        first, second, own = adam(params[s], adam_m[s], adam_v[s], total.T)
        inner[s] = own
        c_copy(c).start()
        first_out[s] = first
        second_out[s] = second
        store(c, 0).start()
        store(c, 1).start()

    def join(c):
        c_copy(c).wait_recv()
        y_out[c] = inner[piece(c)] + core_in[c]
        for e in range(1, pairs):
            for k in range(2):
                y_copy(c, e, k).start()

    def outer(c):
        for e in range(1, pairs):
            for k in range(2):
                y_recv(c, e, k).wait_recv()
        for k in range(2):
            s = pl.ds(c * step + k * half, half)
            summed = y_out[c, pl.ds(k * half, half)]
            for e in range(1, pairs):
                summed = summed + y_in[c, e, k]
            delta = global_params[s] - summed / (2 * pairs)
            fresh = momentum * outer_mom[s] + delta
            moved = global_params[s] - outer_rate * (delta + momentum * fresh)
            merged = mixing * inner[s] + (1.0 - mixing) * moved
            first = pl.multiple_of(me * rows + c * step + k * half, half)
            forward[pl.ds(first, half)] = merged.astype(jnp.bfloat16)
            mixed[s] = merged
            new_mom[s] = fresh
            new_global[s] = moved
        for q in range(2):
            g_copy(c, q, 0, 0).start()
        keep(c, 0, 0).start()
        for n in range(2, 5):
            store(c, n).start()

    def pass_on(c, q, s):
        g_copy(c, q, s - 1, s).wait_recv()
        g_copy(c, q, s, s).start()
        keep(c, q, s).start()

    def tick(c, t):
        if t < depth:
            for q in range(2):
                if t < reach(c, q):
                    sum_on(c, q, t)
        elif t == depth:
            reduce(c)
        elif t == depth + 1:
            join(c)
        elif t == depth + 2:
            outer(c)
        else:
            for q in range(2):
                if t - depth - 2 < reach(c, q):
                    pass_on(c, q, t - depth - 2)

    inputs[0].wait()
    turned[...] = grad_out[...].T
    product(depth)
    pl.semaphore_wait(barrier, len(peers))
    for far in (depth, depth - 1):
        if far < depth:
            product(far)
            product(ring - far)
        for c in range(chunks):
            for q in range(2):
                if lags[c] == 0 and reach(c, q) == far:
                    sum_on(c, q, 0)
    for t in range(1, 2 * depth + 2 + max(lags)):
        if t < depth - 1:
            product(depth - 1 - t)
            product(depth + 1 + t)
        elif t == depth - 1:
            product(0)
            for copy in inputs[1:]:
                copy.wait()
        for c in range(chunks):
            if 0 <= t - lags[c] < 2 * depth + 2:
                tick(c, t - lags[c])

    for c in range(chunks):
        c_copy(c).wait_send()
        for e in range(1, pairs):
            for k in range(2):
                y_copy(c, e, k).wait_send()
        for q in range(2):
            for s in range(reach(c, q)):
                r_copy(c, q, s).wait_send()
                g_copy(c, q, s, s).wait_send()
            g_copy(c, q, reach(c, q) - 1, reach(c, q)).wait_recv()
            keep(c, q, reach(c, q)).start()
    for c in range(chunks):
        for n in range(5):
            store(c, n).wait()
        keep(c, 0, 0).wait()
        for q in range(2):
            for hop in range(1, reach(c, q) + 1):
                keep(c, q, hop).wait()


def write_out(parts, *refs):
    count = len(parts)
    sources, targets, held = refs[:count], refs[count : 2 * count], refs[2 * count : 3 * count]
    in_sem, out_sem = refs[3 * count :]
    loads, stores = [], []
    for n, cuts in enumerate(parts):
        extent = sources[n].shape[0] // cuts
        for cut in range(cuts):
            at = pl.ds(cut * extent, extent)
            spot = len(loads)
            loads.append(
                pltpu.make_async_copy(sources[n].at[at], held[n].at[at], in_sem.at[spot])
            )
            stores.append(
                pltpu.make_async_copy(held[n].at[at], targets[n].at[at], out_sem.at[spot])
            )
    for copy in loads:
        copy.start()
    for load, store in zip(loads, stores):
        load.wait()
        store.start()
    for copy in stores:
        copy.wait()


def fused(acts, grad_out, params, adam_m, adam_v, global_params, outer_mom):
    ring, islands = lax.axis_size("fsdp"), lax.axis_size("island")
    depth, pairs = ring // 2, islands // 2
    rows, width = params.shape[1:]
    tokens = acts.shape[1]
    chunks = len(LAGS)
    step = rows // chunks
    single = jax.ShapeDtypeStruct((rows, width), jnp.float32)
    whole = jax.ShapeDtypeStruct((ring * rows, width), jnp.bfloat16)
    dma = pltpu.SemaphoreType.DMA
    hbm = pl.BlockSpec(memory_space=pltpu.HBM)
    own = pltpu.VMEM((rows, width), jnp.float32)
    coded = pltpu.VMEM((chunks, 2, depth, width, step), jnp.bfloat16)
    results = pl.pallas_call(
        functools.partial(kernel, ring, pairs, chunks, LAGS),
        out_shape=[single] * 5 + [whole],
        in_specs=[hbm] * 7,
        out_specs=[hbm] * 6,
        scratch_shapes=[
            own, own, own, own, own,
            pltpu.VMEM((ring * rows, width), jnp.bfloat16),
            pltpu.VMEM((ring, tokens, rows), jnp.bfloat16),
            pltpu.VMEM((tokens, width), jnp.bfloat16),
            own, own, own, own, own,
            pltpu.VMEM((width, tokens), jnp.bfloat16),
            pltpu.VMEM((ring, width, rows), jnp.float32),
            coded, coded,
            own,
            pltpu.VMEM((chunks, step, width), jnp.float32),
            pltpu.VMEM((chunks, step, width), jnp.float32),
            pltpu.VMEM((chunks, pairs, 2, step // 2, width), jnp.float32),
            dma((ring,)), dma((6,)), dma((chunks, 5)), dma((chunks, 2, depth + 1)),
            dma((chunks, 2, depth)), dma((chunks, 2, depth)),
            dma((chunks,)), dma((chunks,)),
            dma((chunks, pairs, 2)), dma((chunks, pairs, 2)),
            dma((chunks, 2, depth)), dma((chunks, 2, depth)),
        ],
        compiler_params=pltpu.CompilerParams(
            collective_id=0, has_side_effects=True, vmem_limit_bytes=VMEM_LIMIT
        ),
    )(acts[0], grad_out[0], params[0], adam_m[0], adam_v[0], global_params, outer_mom)
    parts = (1,) * 5 + (4,)
    mixed, first, second, new_global, new_mom, forward = pl.pallas_call(
        functools.partial(write_out, parts),
        out_shape=[single] * 5 + [whole],
        in_specs=[hbm] * 6,
        out_specs=[hbm] * 6,
        scratch_shapes=[own] * 5 + [pltpu.VMEM(whole.shape, whole.dtype)] + [dma((sum(parts),))] * 2,
        compiler_params=pltpu.CompilerParams(vmem_limit_bytes=VMEM_LIMIT),
    )(*results)
    return mixed[None], first[None], second[None], new_global, new_mom, forward[None]


def general(acts, grad_out, params, adam_m, adam_v, global_params, outer_mom):
    shard_rows = params.shape[1]
    features = acts.shape[2]
    padded_rows = shard_rows * lax.axis_size("fsdp")
    islands = lax.axis_size("island")
    inputs = acts[0]
    cotangent = grad_out[0]
    whole = jnp.einsum("td,th->dh", inputs, cotangent, preferred_element_type=jnp.float32)
    whole = jnp.pad(whole, ((0, padded_rows - features), (0, 0)))
    gradient = lax.psum_scatter(whole, "fsdp", scatter_dimension=0, tiled=True)
    first_moment, second_moment, inner = adam(params, adam_m, adam_v, gradient[None])
    summed = lax.psum(inner, "island")
    delta = global_params - summed[0] / islands
    new_mom = momentum * outer_mom + delta
    new_global = global_params - outer_rate * (delta + momentum * new_mom)
    mixed = mixing * inner + (1.0 - mixing) * new_global[None]
    gathered = lax.all_gather(mixed.astype(jnp.bfloat16), "fsdp", axis=1, tiled=True)
    forward_weight = gathered[:, :features]
    return (mixed, first_moment, second_moment, new_global, new_mom, forward_weight)


def on_device(acts, *others):
    fsdp, islands = lax.axis_size("fsdp"), lax.axis_size("island")
    rows = others[1].shape[1]
    fits = (
        rows * fsdp == acts.shape[2]
        and rows % (len(LAGS) * 128) == 0
        and fsdp % 2 == 0
        and 2 <= fsdp // 2 <= 4
        and islands == 4
    )
    return (fused if fits else general)(acts, *others)


def solution(mesh):
    in_specs = (
        P("island", "fsdp", None),
        P("island", "fsdp", None),
        P("island", "fsdp", None),
        P("island", "fsdp", None),
        P("island", "fsdp", None),
        P("fsdp", None),
        P("fsdp", None),
    )
    out_specs = (
        P("island", "fsdp", None),
        P("island", "fsdp", None),
        P("island", "fsdp", None),
        P("fsdp", None),
        P("fsdp", None),
        P("island", None, None),
    )
    return jax.shard_map(
        on_device, mesh=mesh, in_specs=in_specs, out_specs=out_specs, check_vma=False
    )
```

```python
import functools

import jax
import jax.numpy as jnp
from jax import lax
from jax.experimental import pallas as pl
from jax.experimental.pallas import tpu as pltpu
from jax.sharding import PartitionSpec as P

INNER_STEP = 100


beta_one = 0.9
beta_two = 0.95
epsilon = 1e-08
inner_rate = 0.001
decay_rate = 0.1
outer_rate = 0.7
momentum = 0.9
mixing = 0.5

CODE_SCALE = 4096.0
LAGS = (0, 0, 0, 0)
VMEM_LIMIT = 60 * 2**20


def encode(value):
    scaled = value * CODE_SCALE
    return (scaled * jnp.abs(scaled) * (scaled * scaled)).astype(jnp.bfloat16)


def decode(coded):
    wide = coded.astype(jnp.float32)
    size = jnp.maximum(jnp.abs(wide), 1e-37)
    root = lax.rsqrt(lax.rsqrt(size)) * (1.0 / CODE_SCALE)
    return jnp.where(wide < 0.0, -root, root)


def adam(params, adam_m, adam_v, gradient):
    first_moment = beta_one * adam_m + (1.0 - beta_one) * gradient
    second_moment = beta_two * adam_v + (1.0 - beta_two) * gradient * gradient
    first_hat = first_moment / (1.0 - beta_one**INNER_STEP)
    second_hat = second_moment / (1.0 - beta_two**INNER_STEP)
    inner = params - inner_rate * (
        first_hat / (jnp.sqrt(second_hat) + epsilon) + decay_rate * params
    )
    return first_moment, second_moment, inner


def kernel(
    ring, pairs, chunks, lags,
    acts_hbm, grad_hbm, params_hbm, m_hbm, v_hbm, global_hbm, mom_hbm,
    mixed_hbm, first_hbm, second_hbm, new_global_hbm, new_mom_hbm, forward_hbm,
    mixed, first_out, second_out, new_global, new_mom, forward,
    acts, grad_out, params, adam_m, adam_v, global_params, outer_mom,
    turned, part, r_out, r_in, inner, core_in, y_out, y_in, y_sum,
    a_sem, i_sem, o_sem, w_sem, r_ss, r_rs, c_ss, c_rs, y_ss, y_rs, m_ss, m_rs, g_ss, g_rs,
):
    rows = params.shape[0]
    step = rows // chunks
    half = step // 2
    depth = ring // 2
    me = lax.axis_index("fsdp")
    isle = lax.axis_index("island")
    zi, xi = me // 2, lax.rem(me, 2)
    place = zi * (1 - xi) + (ring - 1 - zi) * xi
    pair, core = isle // 2, lax.rem(isle, 2)

    def index(k):
        spot = lax.rem(place + (k % ring), ring)
        side = spot // depth
        return (spot * (1 - side) + (ring - 1 - spot) * side) * 2 + side

    ahead = {"fsdp": index(1), "island": isle}
    behind = {"fsdp": index(-1), "island": isle}
    mate = {"fsdp": me, "island": pair * 2 + 1 - core}
    toward = (ahead, behind)

    def across(e):
        return {"fsdp": me, "island": lax.rem(pair + e, pairs) * 2 + core}

    barrier = pltpu.get_barrier_semaphore()
    peers = [ahead, behind, mate] + [across(e) for e in range(1, pairs)]
    for peer in peers:
        pl.semaphore_signal(barrier, inc=1, device_id=peer, device_id_type=pl.DeviceIdType.MESH)

    def columns(k):
        return pl.ds(pl.multiple_of(index(k) * rows, rows), rows)

    def load(k):
        return pltpu.make_async_copy(
            acts_hbm.at[:, columns(k)], acts.at[k % ring], a_sem.at[k % ring]
        )

    singles = [
        (grad_hbm, grad_out), (params_hbm, params), (m_hbm, adam_m), (v_hbm, adam_v),
        (global_hbm, global_params), (mom_hbm, outer_mom),
    ]
    inputs = [pltpu.make_async_copy(s, d, i_sem.at[n]) for n, (s, d) in enumerate(singles)]
    needs = [depth]
    for k in range(depth - 1, 0, -1):
        needs += [k, ring - k]
    needs.append(0)
    inputs[0].start()
    for k in needs:
        load(k).start()
    for copy in inputs[1:]:
        copy.start()

    def product(k):
        load(k).wait()
        part[k] = jnp.dot(turned[...], acts[k], preferred_element_type=jnp.float32)

    def remote(src, dst, ss, rs, where):
        return pltpu.make_async_remote_copy(
            src_ref=src, dst_ref=dst, send_sem=ss, recv_sem=rs,
            device_id=where, device_id_type=pl.DeviceIdType.MESH,
        )

    def reach(c, q):
        return depth - (c + q) % 2

    def piece(c):
        return pl.ds(c * step, step)

    def r_copy(c, q, s):
        return remote(
            r_out.at[c, q, s], r_in.at[c, q, s], r_ss.at[c, q, s], r_rs.at[c, q, s], toward[q]
        )

    def c_copy(c):
        return remote(inner.at[piece(c)], core_in.at[c], c_ss.at[c], c_rs.at[c], mate)

    def my_half():
        return pl.ds(pl.multiple_of(core * half, half), half)

    def y_copy(c, e):
        return remote(
            y_out.at[c, my_half()], y_in.at[c, e], y_ss.at[c, e], y_rs.at[c, e], across(e)
        )

    def m_copy(c):
        block = y_sum.at[c, my_half()]
        return remote(block, block, m_ss.at[c], m_rs.at[c], mate)

    def g_copy(c, q, s, hop):
        k = hop if q else -hop
        first = pl.multiple_of(index(k) * rows + c * step, step)
        block = forward.at[pl.ds(first, step)]
        return remote(block, block, g_ss.at[c, q, s], g_rs.at[c, q, s], toward[q])

    landing = (
        (first_out, first_hbm), (second_out, second_hbm),
        (mixed, mixed_hbm), (new_global, new_global_hbm), (new_mom, new_mom_hbm),
    )

    def store(c, n):
        src, dst = landing[n]
        return pltpu.make_async_copy(src.at[piece(c)], dst.at[piece(c)], o_sem.at[c, n])

    def keep(c, q, hop):
        first = pl.multiple_of(index(hop if q else -hop) * rows + c * step, step)
        place_of = pl.ds(first, step)
        return pltpu.make_async_copy(
            forward.at[place_of], forward_hbm.at[place_of], w_sem.at[c, q, hop]
        )

    def sum_on(c, q, s):
        k = reach(c, q) - s
        value = part[(-k if q else k) % ring, :, piece(c)]
        if s > 0:
            r_copy(c, q, s - 1).wait_recv()
            value = value + decode(r_in[c, q, s - 1])
        r_out[c, q, s] = encode(value)
        r_copy(c, q, s).start()

    def reduce(c):
        total = part[0, :, piece(c)]
        for q in range(2):
            last = reach(c, q) - 1
            r_copy(c, q, last).wait_recv()
            total = total + decode(r_in[c, q, last])
        s = piece(c)
        first, second, own = adam(params[s], adam_m[s], adam_v[s], total.T)
        inner[s] = own
        c_copy(c).start()
        first_out[s] = first
        second_out[s] = second
        store(c, 0).start()
        store(c, 1).start()

    def join(c):
        c_copy(c).wait_recv()
        y_out[c] = inner[piece(c)] + core_in[c]
        for e in range(1, pairs):
            y_copy(c, e).start()

    def swap(c):
        total = y_out[c, my_half()]
        for e in range(1, pairs):
            y_copy(c, e).wait_recv()
            total = total + y_in[c, e]
        y_sum[c, my_half()] = total
        m_copy(c).start()

    def outer(c):
        m_copy(c).wait_recv()
        for k in range(2):
            s = pl.ds(c * step + k * half, half)
            summed = y_sum[c, pl.ds(k * half, half)]
            delta = global_params[s] - summed / (2 * pairs)
            fresh = momentum * outer_mom[s] + delta
            moved = global_params[s] - outer_rate * (delta + momentum * fresh)
            merged = mixing * inner[s] + (1.0 - mixing) * moved
            first = pl.multiple_of(me * rows + c * step + k * half, half)
            forward[pl.ds(first, half)] = merged.astype(jnp.bfloat16)
            mixed[s] = merged
            new_mom[s] = fresh
            new_global[s] = moved
        for q in range(2):
            g_copy(c, q, 0, 0).start()
        keep(c, 0, 0).start()
        for n in range(2, 5):
            store(c, n).start()

    def pass_on(c, q, s):
        g_copy(c, q, s - 1, s).wait_recv()
        g_copy(c, q, s, s).start()
        keep(c, q, s).start()

    def tick(c, t):
        if t < depth:
            for q in range(2):
                if t < reach(c, q):
                    sum_on(c, q, t)
        elif t == depth:
            reduce(c)
        elif t == depth + 1:
            join(c)
        elif t == depth + 2:
            swap(c)
        elif t == depth + 3:
            outer(c)
        else:
            for q in range(2):
                if t - depth - 3 < reach(c, q):
                    pass_on(c, q, t - depth - 3)

    inputs[0].wait()
    turned[...] = grad_out[...].T
    product(depth)
    pl.semaphore_wait(barrier, len(peers))
    for far in (depth, depth - 1):
        if far < depth:
            product(far)
            product(ring - far)
        for c in range(chunks):
            for q in range(2):
                if lags[c] == 0 and reach(c, q) == far:
                    sum_on(c, q, 0)
    for t in range(1, 2 * depth + 3 + max(lags)):
        if t < depth - 1:
            product(depth - 1 - t)
            product(depth + 1 + t)
        elif t == depth - 1:
            product(0)
            for copy in inputs[1:]:
                copy.wait()
        for c in range(chunks):
            if 0 <= t - lags[c] < 2 * depth + 3:
                tick(c, t - lags[c])
        for c in range(chunks):
            if t == depth + 4 + max(lags):
                for q in range(2):
                    for s in range(reach(c, q)):
                        r_copy(c, q, s).wait_send()
            if t == depth + 5 + max(lags):
                c_copy(c).wait_send()
                m_copy(c).wait_send()
                for e in range(1, pairs):
                    y_copy(c, e).wait_send()
                for n in range(5):
                    store(c, n).wait()
                keep(c, 0, 0).wait()
            if t == 2 * depth + 2 + max(lags):
                for q in range(2):
                    for s in range(reach(c, q) - 2):
                        g_copy(c, q, s, s).wait_send()
                        keep(c, q, s + 1).wait()

    for c in range(chunks):
        for q in range(2):
            g_copy(c, q, reach(c, q) - 1, reach(c, q)).wait_recv()
            keep(c, q, reach(c, q)).start()
    for c in range(chunks):
        for q in range(2):
            for s in range(reach(c, q) - 2, reach(c, q)):
                g_copy(c, q, s, s).wait_send()
                keep(c, q, s + 1).wait()


def write_out(parts, *refs):
    count = len(parts)
    sources, targets, held = refs[:count], refs[count : 2 * count], refs[2 * count : 3 * count]
    in_sem, out_sem = refs[3 * count :]
    loads, stores = [], []
    for n, cuts in enumerate(parts):
        extent = sources[n].shape[0] // cuts
        for cut in range(cuts):
            at = pl.ds(cut * extent, extent)
            spot = len(loads)
            loads.append(
                pltpu.make_async_copy(sources[n].at[at], held[n].at[at], in_sem.at[spot])
            )
            stores.append(
                pltpu.make_async_copy(held[n].at[at], targets[n].at[at], out_sem.at[spot])
            )
    for copy in loads:
        copy.start()
    for load, store in zip(loads, stores):
        load.wait()
        store.start()
    for copy in stores:
        copy.wait()


def fused(acts, grad_out, params, adam_m, adam_v, global_params, outer_mom):
    ring, islands = lax.axis_size("fsdp"), lax.axis_size("island")
    depth, pairs = ring // 2, islands // 2
    rows, width = params.shape[1:]
    tokens = acts.shape[1]
    chunks = len(LAGS)
    step = rows // chunks
    single = jax.ShapeDtypeStruct((rows, width), jnp.float32)
    whole = jax.ShapeDtypeStruct((ring * rows, width), jnp.bfloat16)
    dma = pltpu.SemaphoreType.DMA
    hbm = pl.BlockSpec(memory_space=pltpu.HBM)
    own = pltpu.VMEM((rows, width), jnp.float32)
    coded = pltpu.VMEM((chunks, 2, depth, width, step), jnp.bfloat16)
    results = pl.pallas_call(
        functools.partial(kernel, ring, pairs, chunks, LAGS),
        out_shape=[single] * 5 + [whole],
        in_specs=[hbm] * 7,
        out_specs=[hbm] * 6,
        scratch_shapes=[
            own, own, own, own, own,
            pltpu.VMEM((ring * rows, width), jnp.bfloat16),
            pltpu.VMEM((ring, tokens, rows), jnp.bfloat16),
            pltpu.VMEM((tokens, width), jnp.bfloat16),
            own, own, own, own, own,
            pltpu.VMEM((width, tokens), jnp.bfloat16),
            pltpu.VMEM((ring, width, rows), jnp.float32),
            coded, coded,
            own,
            pltpu.VMEM((chunks, step, width), jnp.float32),
            pltpu.VMEM((chunks, step, width), jnp.float32),
            pltpu.VMEM((chunks, pairs, step // 2, width), jnp.float32),
            pltpu.VMEM((chunks, step, width), jnp.float32),
            dma((ring,)), dma((6,)), dma((chunks, 5)), dma((chunks, 2, depth + 1)),
            dma((chunks, 2, depth)), dma((chunks, 2, depth)),
            dma((chunks,)), dma((chunks,)),
            dma((chunks, pairs)), dma((chunks, pairs)),
            dma((chunks,)), dma((chunks,)),
            dma((chunks, 2, depth)), dma((chunks, 2, depth)),
        ],
        compiler_params=pltpu.CompilerParams(
            collective_id=0, has_side_effects=True, vmem_limit_bytes=VMEM_LIMIT
        ),
    )(acts[0], grad_out[0], params[0], adam_m[0], adam_v[0], global_params, outer_mom)
    parts = (1,) * 5 + (4,)
    mixed, first, second, new_global, new_mom, forward = pl.pallas_call(
        functools.partial(write_out, parts),
        out_shape=[single] * 5 + [whole],
        in_specs=[hbm] * 6,
        out_specs=[hbm] * 6,
        scratch_shapes=[own] * 5 + [pltpu.VMEM(whole.shape, whole.dtype)] + [dma((sum(parts),))] * 2,
        compiler_params=pltpu.CompilerParams(vmem_limit_bytes=VMEM_LIMIT),
    )(*results)
    return mixed[None], first[None], second[None], new_global, new_mom, forward[None]


def general(acts, grad_out, params, adam_m, adam_v, global_params, outer_mom):
    shard_rows = params.shape[1]
    features = acts.shape[2]
    padded_rows = shard_rows * lax.axis_size("fsdp")
    islands = lax.axis_size("island")
    inputs = acts[0]
    cotangent = grad_out[0]
    whole = jnp.einsum("td,th->dh", inputs, cotangent, preferred_element_type=jnp.float32)
    whole = jnp.pad(whole, ((0, padded_rows - features), (0, 0)))
    gradient = lax.psum_scatter(whole, "fsdp", scatter_dimension=0, tiled=True)
    first_moment, second_moment, inner = adam(params, adam_m, adam_v, gradient[None])
    summed = lax.psum(inner, "island")
    delta = global_params - summed[0] / islands
    new_mom = momentum * outer_mom + delta
    new_global = global_params - outer_rate * (delta + momentum * new_mom)
    mixed = mixing * inner + (1.0 - mixing) * new_global[None]
    gathered = lax.all_gather(mixed.astype(jnp.bfloat16), "fsdp", axis=1, tiled=True)
    forward_weight = gathered[:, :features]
    return (mixed, first_moment, second_moment, new_global, new_mom, forward_weight)


def on_device(acts, *others):
    fsdp, islands = lax.axis_size("fsdp"), lax.axis_size("island")
    rows = others[1].shape[1]
    fits = (
        rows * fsdp == acts.shape[2]
        and rows % (len(LAGS) * 128) == 0
        and fsdp % 2 == 0
        and 3 <= fsdp // 2 <= 4
        and islands == 4
    )
    return (fused if fits else general)(acts, *others)


def solution(mesh):
    in_specs = (
        P("island", "fsdp", None),
        P("island", "fsdp", None),
        P("island", "fsdp", None),
        P("island", "fsdp", None),
        P("island", "fsdp", None),
        P("fsdp", None),
        P("fsdp", None),
    )
    out_specs = (
        P("island", "fsdp", None),
        P("island", "fsdp", None),
        P("island", "fsdp", None),
        P("fsdp", None),
        P("fsdp", None),
        P("island", None, None),
    )
    return jax.shard_map(
        on_device, mesh=mesh, in_specs=in_specs, out_specs=out_specs, check_vma=False
    )
```

```python
import functools

import jax
import jax.numpy as jnp
from jax import lax
from jax.experimental import pallas as pl
from jax.experimental.pallas import tpu as pltpu
from jax.sharding import PartitionSpec as P

INNER_STEP = 100


beta_one = 0.9
beta_two = 0.95
epsilon = 1e-08
inner_rate = 0.001
decay_rate = 0.1
outer_rate = 0.7
momentum = 0.9
mixing = 0.5

CODE_SCALE = 4096.0
LAGS = (0, 0)
VMEM_LIMIT = 60 * 2**20


def encode(value):
    scaled = value * CODE_SCALE
    return (scaled * jnp.abs(scaled) * (scaled * scaled)).astype(jnp.bfloat16)


def decode(coded):
    wide = coded.astype(jnp.float32)
    size = jnp.maximum(jnp.abs(wide), 1e-37)
    root = lax.rsqrt(lax.rsqrt(size)) * (1.0 / CODE_SCALE)
    return jnp.where(wide < 0.0, -root, root)


def adam(params, adam_m, adam_v, gradient):
    first_moment = beta_one * adam_m + (1.0 - beta_one) * gradient
    second_moment = beta_two * adam_v + (1.0 - beta_two) * gradient * gradient
    first_hat = first_moment / (1.0 - beta_one**INNER_STEP)
    second_hat = second_moment / (1.0 - beta_two**INNER_STEP)
    inner = params - inner_rate * (
        first_hat / (jnp.sqrt(second_hat) + epsilon) + decay_rate * params
    )
    return first_moment, second_moment, inner


def kernel(
    ring, pairs, chunks, lags,
    acts_hbm, grad_hbm, params_hbm, m_hbm, v_hbm, global_hbm, mom_hbm,
    mixed_hbm, first_hbm, second_hbm, new_global_hbm, new_mom_hbm, forward_hbm,
    mixed, first_out, second_out, new_global, new_mom, forward,
    acts, grad_out, params, adam_m, adam_v, global_params, outer_mom,
    turned, part, r_out, r_in, inner, core_in, y_out, y_in, y_sum,
    a_sem, i_sem, o_sem, w_sem, r_ss, r_rs, c_ss, c_rs, y_ss, y_rs, m_ss, m_rs, g_ss, g_rs,
):
    rows = params.shape[0]
    step = rows // chunks
    half = step // 2
    depth = ring // 2
    me = lax.axis_index("fsdp")
    isle = lax.axis_index("island")
    zi, xi = me // 2, lax.rem(me, 2)
    place = zi * (1 - xi) + (ring - 1 - zi) * xi
    pair, core = isle // 2, lax.rem(isle, 2)

    def index(k):
        spot = lax.rem(place + (k % ring), ring)
        side = spot // depth
        return (spot * (1 - side) + (ring - 1 - spot) * side) * 2 + side

    ahead = {"fsdp": index(1), "island": isle}
    behind = {"fsdp": index(-1), "island": isle}
    mate = {"fsdp": me, "island": pair * 2 + 1 - core}
    toward = (ahead, behind)

    def across(e):
        return {"fsdp": me, "island": lax.rem(pair + e, pairs) * 2 + core}

    barrier = pltpu.get_barrier_semaphore()
    peers = [ahead, behind, mate] + [across(e) for e in range(1, pairs)]
    for peer in peers:
        pl.semaphore_signal(barrier, inc=1, device_id=peer, device_id_type=pl.DeviceIdType.MESH)

    def columns(k):
        return pl.ds(pl.multiple_of(index(k) * rows, rows), rows)

    def load(k):
        return pltpu.make_async_copy(
            acts_hbm.at[:, columns(k)], acts.at[k % ring], a_sem.at[k % ring]
        )

    singles = [
        (grad_hbm, grad_out), (params_hbm, params), (m_hbm, adam_m), (v_hbm, adam_v),
        (global_hbm, global_params), (mom_hbm, outer_mom),
    ]
    inputs = [pltpu.make_async_copy(s, d, i_sem.at[n]) for n, (s, d) in enumerate(singles)]
    needs = [depth]
    for k in range(depth - 1, 0, -1):
        needs += [k, ring - k]
    needs.append(0)
    inputs[0].start()
    for k in needs:
        load(k).start()
    for copy in inputs[1:]:
        copy.start()

    def product(k):
        load(k).wait()
        part[k] = jnp.dot(turned[...], acts[k], preferred_element_type=jnp.float32)

    def remote(src, dst, ss, rs, where):
        return pltpu.make_async_remote_copy(
            src_ref=src, dst_ref=dst, send_sem=ss, recv_sem=rs,
            device_id=where, device_id_type=pl.DeviceIdType.MESH,
        )

    def reach(c, q):
        return depth - (c + q) % 2

    def piece(c):
        return pl.ds(c * step, step)

    def r_copy(c, q, s):
        return remote(
            r_out.at[c, q, s], r_in.at[c, q, s], r_ss.at[c, q, s], r_rs.at[c, q, s], toward[q]
        )

    def c_copy(c):
        return remote(inner.at[piece(c)], core_in.at[c], c_ss.at[c], c_rs.at[c], mate)

    def my_half():
        return pl.ds(pl.multiple_of(core * half, half), half)

    def y_copy(c, e):
        return remote(
            y_out.at[c, my_half()], y_in.at[c, e], y_ss.at[c, e], y_rs.at[c, e], across(e)
        )

    def m_copy(c):
        block = y_sum.at[c, my_half()]
        return remote(block, block, m_ss.at[c], m_rs.at[c], mate)

    def g_copy(c, q, s, hop):
        k = hop if q else -hop
        first = pl.multiple_of(index(k) * rows + c * step, step)
        block = forward.at[pl.ds(first, step)]
        return remote(block, block, g_ss.at[c, q, s], g_rs.at[c, q, s], toward[q])

    landing = (
        (first_out, first_hbm), (second_out, second_hbm),
        (mixed, mixed_hbm), (new_global, new_global_hbm), (new_mom, new_mom_hbm),
    )

    def store(c, n):
        src, dst = landing[n]
        return pltpu.make_async_copy(src.at[piece(c)], dst.at[piece(c)], o_sem.at[c, n])

    def keep(c, q, hop):
        first = pl.multiple_of(index(hop if q else -hop) * rows + c * step, step)
        place_of = pl.ds(first, step)
        return pltpu.make_async_copy(
            forward.at[place_of], forward_hbm.at[place_of], w_sem.at[c, q, hop]
        )

    def sum_on(c, q, s):
        k = reach(c, q) - s
        value = part[(-k if q else k) % ring, :, piece(c)]
        if s > 0:
            r_copy(c, q, s - 1).wait_recv()
            value = value + decode(r_in[c, q, s - 1])
        r_out[c, q, s] = encode(value)
        r_copy(c, q, s).start()

    def reduce(c):
        total = part[0, :, piece(c)]
        for q in range(2):
            last = reach(c, q) - 1
            r_copy(c, q, last).wait_recv()
            total = total + decode(r_in[c, q, last])
        s = piece(c)
        first, second, own = adam(params[s], adam_m[s], adam_v[s], total.T)
        inner[s] = own
        c_copy(c).start()
        first_out[s] = first
        second_out[s] = second
        store(c, 0).start()
        store(c, 1).start()

    def join(c):
        c_copy(c).wait_recv()
        y_out[c] = inner[piece(c)] + core_in[c]
        for e in range(1, pairs):
            y_copy(c, e).start()

    def swap(c):
        total = y_out[c, my_half()]
        for e in range(1, pairs):
            y_copy(c, e).wait_recv()
            total = total + y_in[c, e]
        y_sum[c, my_half()] = total
        m_copy(c).start()

    def outer(c):
        m_copy(c).wait_recv()
        for k in range(2):
            s = pl.ds(c * step + k * half, half)
            summed = y_sum[c, pl.ds(k * half, half)]
            delta = global_params[s] - summed / (2 * pairs)
            fresh = momentum * outer_mom[s] + delta
            moved = global_params[s] - outer_rate * (delta + momentum * fresh)
            merged = mixing * inner[s] + (1.0 - mixing) * moved
            first = pl.multiple_of(me * rows + c * step + k * half, half)
            forward[pl.ds(first, half)] = merged.astype(jnp.bfloat16)
            mixed[s] = merged
            new_mom[s] = fresh
            new_global[s] = moved
        for q in range(2):
            g_copy(c, q, 0, 0).start()
        keep(c, 0, 0).start()
        for n in range(2, 5):
            store(c, n).start()

    def pass_on(c, q, s):
        g_copy(c, q, s - 1, s).wait_recv()
        g_copy(c, q, s, s).start()
        keep(c, q, s).start()

    def tick(c, t):
        if t < depth:
            for q in range(2):
                if t < reach(c, q):
                    sum_on(c, q, t)
        elif t == depth:
            reduce(c)
        elif t == depth + 1:
            join(c)
        elif t == depth + 2:
            swap(c)
        elif t == depth + 3:
            outer(c)
        else:
            for q in range(2):
                if t - depth - 3 < reach(c, q):
                    pass_on(c, q, t - depth - 3)

    inputs[0].wait()
    turned[...] = grad_out[...].T
    product(depth)
    pl.semaphore_wait(barrier, len(peers))
    for far in (depth, depth - 1):
        if far < depth:
            product(far)
            product(ring - far)
        for c in range(chunks):
            for q in range(2):
                if lags[c] == 0 and reach(c, q) == far:
                    sum_on(c, q, 0)
    for t in range(1, 2 * depth + 3 + max(lags)):
        if t < depth - 1:
            product(depth - 1 - t)
            product(depth + 1 + t)
        elif t == depth - 1:
            product(0)
            for copy in inputs[1:]:
                copy.wait()
        for c in range(chunks):
            if 0 <= t - lags[c] < 2 * depth + 3:
                tick(c, t - lags[c])
        for c in range(chunks):
            if t == depth + 4 + max(lags):
                for q in range(2):
                    for s in range(reach(c, q)):
                        r_copy(c, q, s).wait_send()
            if t == depth + 5 + max(lags):
                c_copy(c).wait_send()
                m_copy(c).wait_send()
                for e in range(1, pairs):
                    y_copy(c, e).wait_send()
                for n in range(5):
                    store(c, n).wait()
                keep(c, 0, 0).wait()
            if t == 2 * depth + 2 + max(lags):
                for q in range(2):
                    for s in range(reach(c, q) - 2):
                        g_copy(c, q, s, s).wait_send()
                        keep(c, q, s + 1).wait()

    for c in range(chunks):
        for q in range(2):
            g_copy(c, q, reach(c, q) - 1, reach(c, q)).wait_recv()
            keep(c, q, reach(c, q)).start()
    for c in range(chunks):
        for q in range(2):
            for s in range(reach(c, q) - 2, reach(c, q)):
                g_copy(c, q, s, s).wait_send()
                keep(c, q, s + 1).wait()


def write_out(parts, *refs):
    count = len(parts)
    sources, targets, held = refs[:count], refs[count : 2 * count], refs[2 * count : 3 * count]
    in_sem, out_sem = refs[3 * count :]
    loads, stores = [], []
    for n, cuts in enumerate(parts):
        extent = sources[n].shape[0] // cuts
        for cut in range(cuts):
            at = pl.ds(cut * extent, extent)
            spot = len(loads)
            loads.append(
                pltpu.make_async_copy(sources[n].at[at], held[n].at[at], in_sem.at[spot])
            )
            stores.append(
                pltpu.make_async_copy(held[n].at[at], targets[n].at[at], out_sem.at[spot])
            )
    for copy in loads:
        copy.start()
    for load, store in zip(loads, stores):
        load.wait()
        store.start()
    for copy in stores:
        copy.wait()


def fused(acts, grad_out, params, adam_m, adam_v, global_params, outer_mom):
    ring, islands = lax.axis_size("fsdp"), lax.axis_size("island")
    depth, pairs = ring // 2, islands // 2
    rows, width = params.shape[1:]
    tokens = acts.shape[1]
    chunks = len(LAGS)
    step = rows // chunks
    single = jax.ShapeDtypeStruct((rows, width), jnp.float32)
    whole = jax.ShapeDtypeStruct((ring * rows, width), jnp.bfloat16)
    dma = pltpu.SemaphoreType.DMA
    hbm = pl.BlockSpec(memory_space=pltpu.HBM)
    own = pltpu.VMEM((rows, width), jnp.float32)
    coded = pltpu.VMEM((chunks, 2, depth, width, step), jnp.bfloat16)
    results = pl.pallas_call(
        functools.partial(kernel, ring, pairs, chunks, LAGS),
        out_shape=[single] * 5 + [whole],
        in_specs=[hbm] * 7,
        out_specs=[hbm] * 6,
        scratch_shapes=[
            own, own, own, own, own,
            pltpu.VMEM((ring * rows, width), jnp.bfloat16),
            pltpu.VMEM((ring, tokens, rows), jnp.bfloat16),
            pltpu.VMEM((tokens, width), jnp.bfloat16),
            own, own, own, own, own,
            pltpu.VMEM((width, tokens), jnp.bfloat16),
            pltpu.VMEM((ring, width, rows), jnp.float32),
            coded, coded,
            own,
            pltpu.VMEM((chunks, step, width), jnp.float32),
            pltpu.VMEM((chunks, step, width), jnp.float32),
            pltpu.VMEM((chunks, pairs, step // 2, width), jnp.float32),
            pltpu.VMEM((chunks, step, width), jnp.float32),
            dma((ring,)), dma((6,)), dma((chunks, 5)), dma((chunks, 2, depth + 1)),
            dma((chunks, 2, depth)), dma((chunks, 2, depth)),
            dma((chunks,)), dma((chunks,)),
            dma((chunks, pairs)), dma((chunks, pairs)),
            dma((chunks,)), dma((chunks,)),
            dma((chunks, 2, depth)), dma((chunks, 2, depth)),
        ],
        compiler_params=pltpu.CompilerParams(
            collective_id=0, has_side_effects=True, vmem_limit_bytes=VMEM_LIMIT
        ),
    )(acts[0], grad_out[0], params[0], adam_m[0], adam_v[0], global_params, outer_mom)
    parts = (1,) * 5 + (4,)
    mixed, first, second, new_global, new_mom, forward = pl.pallas_call(
        functools.partial(write_out, parts),
        out_shape=[single] * 5 + [whole],
        in_specs=[hbm] * 6,
        out_specs=[hbm] * 6,
        scratch_shapes=[own] * 5 + [pltpu.VMEM(whole.shape, whole.dtype)] + [dma((sum(parts),))] * 2,
        compiler_params=pltpu.CompilerParams(vmem_limit_bytes=VMEM_LIMIT),
    )(*results)
    return mixed[None], first[None], second[None], new_global, new_mom, forward[None]


def general(acts, grad_out, params, adam_m, adam_v, global_params, outer_mom):
    shard_rows = params.shape[1]
    features = acts.shape[2]
    padded_rows = shard_rows * lax.axis_size("fsdp")
    islands = lax.axis_size("island")
    inputs = acts[0]
    cotangent = grad_out[0]
    whole = jnp.einsum("td,th->dh", inputs, cotangent, preferred_element_type=jnp.float32)
    whole = jnp.pad(whole, ((0, padded_rows - features), (0, 0)))
    gradient = lax.psum_scatter(whole, "fsdp", scatter_dimension=0, tiled=True)
    first_moment, second_moment, inner = adam(params, adam_m, adam_v, gradient[None])
    summed = lax.psum(inner, "island")
    delta = global_params - summed[0] / islands
    new_mom = momentum * outer_mom + delta
    new_global = global_params - outer_rate * (delta + momentum * new_mom)
    mixed = mixing * inner + (1.0 - mixing) * new_global[None]
    gathered = lax.all_gather(mixed.astype(jnp.bfloat16), "fsdp", axis=1, tiled=True)
    forward_weight = gathered[:, :features]
    return (mixed, first_moment, second_moment, new_global, new_mom, forward_weight)


def on_device(acts, *others):
    fsdp, islands = lax.axis_size("fsdp"), lax.axis_size("island")
    rows = others[1].shape[1]
    fits = (
        rows * fsdp == acts.shape[2]
        and rows % (len(LAGS) * 128) == 0
        and fsdp % 2 == 0
        and 3 <= fsdp // 2 <= 4
        and islands == 4
    )
    return (fused if fits else general)(acts, *others)


def solution(mesh):
    in_specs = (
        P("island", "fsdp", None),
        P("island", "fsdp", None),
        P("island", "fsdp", None),
        P("island", "fsdp", None),
        P("island", "fsdp", None),
        P("fsdp", None),
        P("fsdp", None),
    )
    out_specs = (
        P("island", "fsdp", None),
        P("island", "fsdp", None),
        P("island", "fsdp", None),
        P("fsdp", None),
        P("fsdp", None),
        P("island", None, None),
    )
    return jax.shard_map(
        on_device, mesh=mesh, in_specs=in_specs, out_specs=out_specs, check_vma=False
    )
```

```python
import functools

import jax
import jax.numpy as jnp
from jax import lax
from jax.experimental import pallas as pl
from jax.experimental.pallas import tpu as pltpu
from jax.sharding import PartitionSpec as P

INNER_STEP = 100


beta_one = 0.9
beta_two = 0.95
epsilon = 1e-08
inner_rate = 0.001
decay_rate = 0.1
outer_rate = 0.7
momentum = 0.9
mixing = 0.5

CODE_SCALE = 4096.0
LAGS = (0, 0, 1, 1)
VMEM_LIMIT = 60 * 2**20


def encode(value):
    scaled = value * CODE_SCALE
    return (scaled * jnp.abs(scaled) * (scaled * scaled)).astype(jnp.bfloat16)


def decode(coded):
    wide = coded.astype(jnp.float32)
    size = jnp.maximum(jnp.abs(wide), 1e-37)
    root = lax.rsqrt(lax.rsqrt(size)) * (1.0 / CODE_SCALE)
    return jnp.where(wide < 0.0, -root, root)


def adam(params, adam_m, adam_v, gradient):
    first_moment = beta_one * adam_m + (1.0 - beta_one) * gradient
    second_moment = beta_two * adam_v + (1.0 - beta_two) * gradient * gradient
    first_hat = first_moment / (1.0 - beta_one**INNER_STEP)
    second_hat = second_moment / (1.0 - beta_two**INNER_STEP)
    inner = params - inner_rate * (
        first_hat / (jnp.sqrt(second_hat) + epsilon) + decay_rate * params
    )
    return first_moment, second_moment, inner


def kernel(
    ring, pairs, chunks, lags,
    acts_hbm, grad_hbm, params_hbm, m_hbm, v_hbm, global_hbm, mom_hbm,
    mixed_hbm, first_hbm, second_hbm, new_global_hbm, new_mom_hbm, forward_hbm,
    mixed, first_out, second_out, new_global, new_mom, forward,
    acts, grad_out, params, adam_m, adam_v, global_params, outer_mom,
    turned, part, r_out, r_in, inner, core_in, y_out, y_in,
    a_sem, i_sem, o_sem, w_sem, r_ss, r_rs, c_ss, c_rs, y_ss, y_rs, g_ss, g_rs,
):
    rows = params.shape[0]
    step = rows // chunks
    half = step // 2
    depth = ring // 2
    me = lax.axis_index("fsdp")
    isle = lax.axis_index("island")
    zi, xi = me // 2, lax.rem(me, 2)
    place = zi * (1 - xi) + (ring - 1 - zi) * xi
    pair, core = isle // 2, lax.rem(isle, 2)

    def index(k):
        spot = lax.rem(place + (k % ring), ring)
        side = spot // depth
        return (spot * (1 - side) + (ring - 1 - spot) * side) * 2 + side

    ahead = {"fsdp": index(1), "island": isle}
    behind = {"fsdp": index(-1), "island": isle}
    mate = {"fsdp": me, "island": pair * 2 + 1 - core}
    toward = (ahead, behind)

    def across(e, k):
        return {"fsdp": me, "island": lax.rem(pair + e, pairs) * 2 + k}

    barrier = pltpu.get_barrier_semaphore()
    peers = [ahead, behind, mate] + [across(e, k) for e in range(1, pairs) for k in range(2)]
    for peer in peers:
        pl.semaphore_signal(barrier, inc=1, device_id=peer, device_id_type=pl.DeviceIdType.MESH)

    def columns(k):
        return pl.ds(pl.multiple_of(index(k) * rows, rows), rows)

    def load(k):
        return pltpu.make_async_copy(
            acts_hbm.at[:, columns(k)], acts.at[k % ring], a_sem.at[k % ring]
        )

    singles = [
        (grad_hbm, grad_out), (params_hbm, params), (m_hbm, adam_m), (v_hbm, adam_v),
        (global_hbm, global_params), (mom_hbm, outer_mom),
    ]
    inputs = [pltpu.make_async_copy(s, d, i_sem.at[n]) for n, (s, d) in enumerate(singles)]
    needs = [depth]
    for k in range(depth - 1, 0, -1):
        needs += [k, ring - k]
    needs.append(0)
    inputs[0].start()
    for k in needs:
        load(k).start()
    for copy in inputs[1:]:
        copy.start()

    def product(k):
        load(k).wait()
        part[k] = jnp.dot(turned[...], acts[k], preferred_element_type=jnp.float32)

    def remote(src, dst, ss, rs, where):
        return pltpu.make_async_remote_copy(
            src_ref=src, dst_ref=dst, send_sem=ss, recv_sem=rs,
            device_id=where, device_id_type=pl.DeviceIdType.MESH,
        )

    def reach(c, q):
        return depth - (c + q) % 2

    def piece(c):
        return pl.ds(c * step, step)

    def r_copy(c, q, s):
        return remote(
            r_out.at[c, q, s], r_in.at[c, q, s], r_ss.at[c, q, s], r_rs.at[c, q, s], toward[q]
        )

    def c_copy(c):
        return remote(inner.at[piece(c)], core_in.at[c], c_ss.at[c], c_rs.at[c], mate)

    def y_copy(c, e, k):
        return remote(
            y_out.at[c, pl.ds(pl.multiple_of(core * half, half), half)],
            y_in.at[c, e, core], y_ss.at[c, e, k], y_rs.at[c, e, core], across(e, k),
        )

    def y_recv(c, e, k):
        return remote(
            y_out.at[c, pl.ds(0, half)], y_in.at[c, e, k],
            y_ss.at[c, e, k], y_rs.at[c, e, k], mate,
        )

    def g_copy(c, q, s, hop):
        k = hop if q else -hop
        first = pl.multiple_of(index(k) * rows + c * step, step)
        block = forward.at[pl.ds(first, step)]
        return remote(block, block, g_ss.at[c, q, s], g_rs.at[c, q, s], toward[q])

    landing = (
        (first_out, first_hbm), (second_out, second_hbm),
        (mixed, mixed_hbm), (new_global, new_global_hbm), (new_mom, new_mom_hbm),
    )

    def store(c, n):
        src, dst = landing[n]
        return pltpu.make_async_copy(src.at[piece(c)], dst.at[piece(c)], o_sem.at[c, n])

    def keep(c, q, hop):
        first = pl.multiple_of(index(hop if q else -hop) * rows + c * step, step)
        place_of = pl.ds(first, step)
        return pltpu.make_async_copy(
            forward.at[place_of], forward_hbm.at[place_of], w_sem.at[c, q, hop]
        )

    def sum_on(c, q, s):
        k = reach(c, q) - s
        value = part[(-k if q else k) % ring, :, piece(c)]
        if s > 0:
            r_copy(c, q, s - 1).wait_recv()
            value = value + decode(r_in[c, q, s - 1])
        r_out[c, q, s] = encode(value)
        r_copy(c, q, s).start()

    def reduce(c):
        total = part[0, :, piece(c)]
        for q in range(2):
            last = reach(c, q) - 1
            r_copy(c, q, last).wait_recv()
            total = total + decode(r_in[c, q, last])
        s = piece(c)
        first, second, own = adam(params[s], adam_m[s], adam_v[s], total.T)
        inner[s] = own
        c_copy(c).start()
        first_out[s] = first
        second_out[s] = second
        store(c, 0).start()
        store(c, 1).start()

    def join(c):
        c_copy(c).wait_recv()
        y_out[c] = inner[piece(c)] + core_in[c]
        for e in range(1, pairs):
            for k in range(2):
                y_copy(c, e, k).start()

    def outer(c):
        for e in range(1, pairs):
            for k in range(2):
                y_recv(c, e, k).wait_recv()
        for k in range(2):
            s = pl.ds(c * step + k * half, half)
            summed = y_out[c, pl.ds(k * half, half)]
            for e in range(1, pairs):
                summed = summed + y_in[c, e, k]
            delta = global_params[s] - summed / (2 * pairs)
            fresh = momentum * outer_mom[s] + delta
            moved = global_params[s] - outer_rate * (delta + momentum * fresh)
            merged = mixing * inner[s] + (1.0 - mixing) * moved
            first = pl.multiple_of(me * rows + c * step + k * half, half)
            forward[pl.ds(first, half)] = merged.astype(jnp.bfloat16)
            mixed[s] = merged
            new_mom[s] = fresh
            new_global[s] = moved
        for q in range(2):
            g_copy(c, q, 0, 0).start()
        keep(c, 0, 0).start()
        for n in range(2, 5):
            store(c, n).start()

    def pass_on(c, q, s):
        g_copy(c, q, s - 1, s).wait_recv()
        g_copy(c, q, s, s).start()
        keep(c, q, s).start()

    def tick(c, t):
        if t < depth:
            for q in range(2):
                if t < reach(c, q):
                    sum_on(c, q, t)
        elif t == depth:
            reduce(c)
        elif t == depth + 1:
            join(c)
        elif t == depth + 2:
            outer(c)
        else:
            for q in range(2):
                if t - depth - 2 < reach(c, q):
                    pass_on(c, q, t - depth - 2)

    inputs[0].wait()
    turned[...] = grad_out[...].T
    product(depth)
    pl.semaphore_wait(barrier, len(peers))
    for far in (depth, depth - 1):
        if far < depth:
            product(far)
            product(ring - far)
        for c in range(chunks):
            for q in range(2):
                if lags[c] == 0 and reach(c, q) == far:
                    sum_on(c, q, 0)
    for t in range(1, 2 * depth + 2 + max(lags)):
        if t < depth - 1:
            product(depth - 1 - t)
            product(depth + 1 + t)
        elif t == depth - 1:
            product(0)
            for copy in inputs[1:]:
                copy.wait()
        for c in range(chunks):
            if 0 <= t - lags[c] < 2 * depth + 2:
                tick(c, t - lags[c])

    for c in range(chunks):
        c_copy(c).wait_send()
        for e in range(1, pairs):
            for k in range(2):
                y_copy(c, e, k).wait_send()
        for q in range(2):
            for s in range(reach(c, q)):
                r_copy(c, q, s).wait_send()
                g_copy(c, q, s, s).wait_send()
            g_copy(c, q, reach(c, q) - 1, reach(c, q)).wait_recv()
            keep(c, q, reach(c, q)).start()
    for c in range(chunks):
        for n in range(5):
            store(c, n).wait()
        keep(c, 0, 0).wait()
        for q in range(2):
            for hop in range(1, reach(c, q) + 1):
                keep(c, q, hop).wait()


def write_out(parts, *refs):
    count = len(parts)
    sources, targets, held = refs[:count], refs[count : 2 * count], refs[2 * count : 3 * count]
    in_sem, out_sem = refs[3 * count :]
    loads, stores = [], []
    for n, cuts in enumerate(parts):
        extent = sources[n].shape[0] // cuts
        for cut in range(cuts):
            at = pl.ds(cut * extent, extent)
            spot = len(loads)
            loads.append(
                pltpu.make_async_copy(sources[n].at[at], held[n].at[at], in_sem.at[spot])
            )
            stores.append(
                pltpu.make_async_copy(held[n].at[at], targets[n].at[at], out_sem.at[spot])
            )
    for copy in loads:
        copy.start()
    for load, store in zip(loads, stores):
        load.wait()
        store.start()
    for copy in stores:
        copy.wait()


def fused(acts, grad_out, params, adam_m, adam_v, global_params, outer_mom):
    ring, islands = lax.axis_size("fsdp"), lax.axis_size("island")
    depth, pairs = ring // 2, islands // 2
    rows, width = params.shape[1:]
    tokens = acts.shape[1]
    chunks = len(LAGS)
    step = rows // chunks
    single = jax.ShapeDtypeStruct((rows, width), jnp.float32)
    whole = jax.ShapeDtypeStruct((ring * rows, width), jnp.bfloat16)
    dma = pltpu.SemaphoreType.DMA
    hbm = pl.BlockSpec(memory_space=pltpu.HBM)
    own = pltpu.VMEM((rows, width), jnp.float32)
    coded = pltpu.VMEM((chunks, 2, depth, width, step), jnp.bfloat16)
    results = pl.pallas_call(
        functools.partial(kernel, ring, pairs, chunks, LAGS),
        out_shape=[single] * 5 + [whole],
        in_specs=[hbm] * 7,
        out_specs=[hbm] * 6,
        scratch_shapes=[
            own, own, own, own, own,
            pltpu.VMEM((ring * rows, width), jnp.bfloat16),
            pltpu.VMEM((ring, tokens, rows), jnp.bfloat16),
            pltpu.VMEM((tokens, width), jnp.bfloat16),
            own, own, own, own, own,
            pltpu.VMEM((width, tokens), jnp.bfloat16),
            pltpu.VMEM((ring, width, rows), jnp.float32),
            coded, coded,
            own,
            pltpu.VMEM((chunks, step, width), jnp.float32),
            pltpu.VMEM((chunks, step, width), jnp.float32),
            pltpu.VMEM((chunks, pairs, 2, step // 2, width), jnp.float32),
            dma((ring,)), dma((6,)), dma((chunks, 5)), dma((chunks, 2, depth + 1)),
            dma((chunks, 2, depth)), dma((chunks, 2, depth)),
            dma((chunks,)), dma((chunks,)),
            dma((chunks, pairs, 2)), dma((chunks, pairs, 2)),
            dma((chunks, 2, depth)), dma((chunks, 2, depth)),
        ],
        compiler_params=pltpu.CompilerParams(
            collective_id=0, has_side_effects=True, vmem_limit_bytes=VMEM_LIMIT
        ),
    )(acts[0], grad_out[0], params[0], adam_m[0], adam_v[0], global_params, outer_mom)
    parts = (1,) * 5 + (4,)
    mixed, first, second, new_global, new_mom, forward = pl.pallas_call(
        functools.partial(write_out, parts),
        out_shape=[single] * 5 + [whole],
        in_specs=[hbm] * 6,
        out_specs=[hbm] * 6,
        scratch_shapes=[own] * 5 + [pltpu.VMEM(whole.shape, whole.dtype)] + [dma((sum(parts),))] * 2,
        compiler_params=pltpu.CompilerParams(vmem_limit_bytes=VMEM_LIMIT),
    )(*results)
    return mixed[None], first[None], second[None], new_global, new_mom, forward[None]


def general(acts, grad_out, params, adam_m, adam_v, global_params, outer_mom):
    shard_rows = params.shape[1]
    features = acts.shape[2]
    padded_rows = shard_rows * lax.axis_size("fsdp")
    islands = lax.axis_size("island")
    inputs = acts[0]
    cotangent = grad_out[0]
    whole = jnp.einsum("td,th->dh", inputs, cotangent, preferred_element_type=jnp.float32)
    whole = jnp.pad(whole, ((0, padded_rows - features), (0, 0)))
    gradient = lax.psum_scatter(whole, "fsdp", scatter_dimension=0, tiled=True)
    first_moment, second_moment, inner = adam(params, adam_m, adam_v, gradient[None])
    summed = lax.psum(inner, "island")
    delta = global_params - summed[0] / islands
    new_mom = momentum * outer_mom + delta
    new_global = global_params - outer_rate * (delta + momentum * new_mom)
    mixed = mixing * inner + (1.0 - mixing) * new_global[None]
    gathered = lax.all_gather(mixed.astype(jnp.bfloat16), "fsdp", axis=1, tiled=True)
    forward_weight = gathered[:, :features]
    return (mixed, first_moment, second_moment, new_global, new_mom, forward_weight)


def on_device(acts, *others):
    fsdp, islands = lax.axis_size("fsdp"), lax.axis_size("island")
    rows = others[1].shape[1]
    fits = (
        rows * fsdp == acts.shape[2]
        and rows % (len(LAGS) * 128) == 0
        and fsdp % 2 == 0
        and 2 <= fsdp // 2 <= 4
        and islands == 4
    )
    return (fused if fits else general)(acts, *others)


def solution(mesh):
    in_specs = (
        P("island", "fsdp", None),
        P("island", "fsdp", None),
        P("island", "fsdp", None),
        P("island", "fsdp", None),
        P("island", "fsdp", None),
        P("fsdp", None),
        P("fsdp", None),
    )
    out_specs = (
        P("island", "fsdp", None),
        P("island", "fsdp", None),
        P("island", "fsdp", None),
        P("fsdp", None),
        P("fsdp", None),
        P("island", None, None),
    )
    return jax.shard_map(
        on_device, mesh=mesh, in_specs=in_specs, out_specs=out_specs, check_vma=False
    )
```
